512 devices in a mesh: tm: 8 (over y), row: 8 (over x, core), col: 8 (over z).
Axes of the slice: x: 4, y: 8, z: 8, core: 2. Of those that a mesh axis runs over, the one named last changes fastest.
Arguments:
- frames: bfloat16 [32, 128, 256, 128], P('tm', 'row', 'col'), may hold values from -6 to 6
- gain_first: float32 [128], replicated, may hold values from 0.1 to 1.9
- weight_first: bfloat16 [3, 3, 3, 128, 128], replicated, may hold values from -0.109375 to 0.109375
- gain_second: float32 [128], replicated, may hold values from 0.1 to 1.9
- weight_second: bfloat16 [3, 3, 3, 128, 128], replicated, may hold values from -0.109375 to 0.109375
Outputs:
- decoded: bfloat16 [32, 128, 256, 128], P('tm', 'row', 'col')
The draws below stay inside these ranges and needn't reach their ends.
All inputs are finite; a program needn't handle non-finite values.
Results may differ from the reference program's by a relative error of at most 0.0065.
Values may be sent and summed in bfloat16 or wider, within the bound.
A program may use at most 64 MiB of HBM per device.

```python
import jax
import jax.numpy as jnp
from jax import lax

C = 128
FR_DEV = 4
FRAMES = 32
HEIGHT = 128
WIDTH = 256


def shard_levels(key, dims, cuts, low, largest):
    factor_of = 1.0
    for axis_at, parts in cuts:
        draws = jax.random.uniform(jax.random.fold_in(jax.random.fold_in(key, 6), axis_at), (parts,), jnp.float32, low / len(cuts), largest / len(cuts))
        factor_of = factor_of * jnp.repeat(jnp.exp(draws), dims[axis_at] // parts).reshape((-1,) + (1,) * (len(dims) - 1 - axis_at))
    return factor_of


def normal_values(own_key, dims, width, limit, shards=(), kind=jnp.bfloat16):
    drawn = width * jax.random.normal(own_key, dims, jnp.float32)
    if shards:
        drawn = drawn * shard_levels(own_key, dims, shards, -0.22, 0.18)
    return jnp.clip(drawn, -limit, limit).astype(kind)


def setup_inputs(seed: int = 0) -> dict:
    splits = jax.random.split(jax.random.key(seed), 6)
    frames = normal_values(splits[0], (FRAMES, HEIGHT, WIDTH, C), 1.0, 6.0, ((0, 8), (1, 8), (2, 8)))
    gain_first = jnp.clip(1.0 + 0.18 * jax.random.normal(splits[1], (C,), jnp.float32), 0.1, 1.9)
    weight_first = normal_values(splits[2], (3, 3, 3, C, C), (27 * C) ** -0.5, 0.109375)
    gain_second = jnp.clip(1.0 + 0.18 * jax.random.normal(splits[3], (C,), jnp.float32), 0.1, 1.9)
    weight_second = normal_values(splits[4], (3, 3, 3, C, C), (27 * C) ** -0.5, 0.109375)
    return dict(frames=frames, gain_first=gain_first, weight_first=weight_first, gain_second=gain_second, weight_second=weight_second)


def normed(values, gain):
    v = values.astype(jnp.float32)
    scaled = v * lax.rsqrt(lax.optimization_barrier(jnp.mean(v * v, axis=-1, keepdims=True)) + 1e-06) * gain
    return jax.nn.silu(scaled).astype(jnp.bfloat16)

def convolve(active, weight):
    padded = jnp.pad(active, ((2, 0), (1, 1), (1, 1), (0, 0)))
    kernel = weight.astype(jnp.float32)
    blocks = FRAMES // FR_DEV

    def one_block(index):
        piece = lax.dynamic_slice_in_dim(padded, index * FR_DEV, FR_DEV + 2, 0).astype(jnp.float32)
        result = lax.conv_general_dilated(piece[None], kernel, (1, 1, 1), 'VALID', dimension_numbers=('NDHWC', 'DHWIO', 'NDHWC'), precision=lax.Precision.HIGHEST)
        return result[0]
    outputs = lax.map(one_block, jnp.arange(blocks, dtype=jnp.int32))
    return outputs.reshape(FRAMES, HEIGHT, WIDTH, C)

def reference(frames, gain_first, weight_first, gain_second, weight_second):
    first = normed(frames, gain_first)
    hidden = convolve(first, weight_first).astype(jnp.bfloat16)
    second = normed(hidden, gain_second)
    total = frames.astype(jnp.float32) + convolve(second, weight_second)
    return total.astype(jnp.bfloat16)
```

```python
import functools

import jax
import jax.numpy as jnp
from jax import lax
from jax.experimental import pallas as pl
from jax.experimental.pallas import tpu as pltpu
from jax.sharding import PartitionSpec as P

MESH = pl.DeviceIdType.MESH
F32, BF16 = jnp.float32, jnp.bfloat16
DIRS = ((-1, 0), (1, 0), (-1, -1), (0, -1), (1, -1), (-1, 1), (0, 1), (1, 1))
PITCH = 48


def act(v, gain):
    half = v * lax.rsqrt(jnp.mean(v * v, axis=-1, keepdims=True) + 1e-6) * (0.5 * gain)
    return half + half * jnp.tanh(half)


def kernel(sizes, T, H, W, C, x_hbm, g1_ref, w1_hbm, g2_ref, w2_hbm, o_ref,
           x_ref, w1, w2, pad1, pad2, s1, s2, acc1, acc2, prev_raw, q_out, q_in,
           sr0, sr1, sr2, sr3, sc0, sc1, sc2, sc3, rr0, rr1, rr2, rr3, rc0, rc1, rc2, rc3,
           local_sem, y_send, y_recv, send_sem, recv_sem):
    at = {a: lax.axis_index(a) for a in ("tm", "row", "col")}
    sends_row, sends_col = (sr0, sr1, sr2, sr3), (sc0, sc1, sc2, sc3)
    recvs_row, recvs_col = (rr0, rr1, rr2, rr3), (rc0, rc1, rc2, rc3)

    def exists(dr, dc):
        r, c = at["row"] + dr, at["col"] + dc
        return (r >= 0) & (r < sizes["row"]) & (c >= 0) & (c < sizes["col"])

    def place(dr, dc):
        return {"row": at["row"] + dr, "col": at["col"] + dc}

    has_next, has_prev = at["tm"] + 1 < sizes["tm"], at["tm"] > 0

    copies = [pltpu.make_async_copy(x_hbm, x_ref, local_sem.at[0])]
    for k, (src, dst) in enumerate(((w1_hbm, w1), (w2_hbm, w2))):
        for kt in range(3):
            copies.append(pltpu.make_async_copy(src.at[kt], dst.at[:, (2 - kt) * C:(3 - kt) * C], local_sem.at[1 + 3 * k + kt]))
    for c in copies:
        c.start()

    for ref in recvs_row + recvs_col + (prev_raw, q_in):
        ref[...] = jnp.zeros_like(ref)

    barrier = pltpu.get_barrier_semaphore()
    expected = has_next.astype(jnp.int32)

    @pl.when(has_prev)
    def _():
        pl.semaphore_signal(barrier, inc=1, device_id={"tm": at["tm"] - 1}, device_id_type=MESH)

    for dr, dc in DIRS:
        @pl.when(exists(dr, dc))
        def _():
            pl.semaphore_signal(barrier, inc=1, device_id=place(dr, dc), device_id_type=MESH)
        expected = expected + exists(dr, dc).astype(jnp.int32)
    pl.semaphore_wait(barrier, expected)

    def y_copy(src, dst, k):
        return pltpu.make_async_remote_copy(
            src_ref=src, dst_ref=dst, send_sem=y_send.at[k], recv_sem=y_recv.at[k],
            device_id={"tm": at["tm"] + 1}, device_id_type=MESH)

    raw_copy = y_copy(x_hbm.at[T - 2:T], prev_raw, 0)
    sum_copy = y_copy(q_out, q_in, 1)

    @pl.when(has_next)
    def _():
        raw_copy.start()

    def rim_copy(k, d):
        dr, dc = DIRS[d]
        if dc == 0:
            src, dst = sends_row[k].at[d], recvs_row[k].at[d]
        else:
            src, dst = sends_col[k].at[0 if dc < 0 else 1], recvs_col[k].at[d - 2]
        return pltpu.make_async_remote_copy(
            src_ref=src, dst_ref=dst, send_sem=send_sem.at[k, d], recv_sem=recv_sem.at[k, d],
            device_id=place(dr, dc), device_id_type=MESH)

    def activate(load, gain, pad, plane):
        def step(i, _):
            for j in range(8):
                h = i * 8 + j
                pad[plane * (H + 2) + 1 + h, 8:8 + W] = act(load(h).astype(F32), gain)
            return 0
        lax.fori_loop(0, H // 8, step, 0)

    def send_rims(k, pad, plane, count):
        flat = pad.reshape(pad.shape[0] * PITCH, C)
        for f in range(count):
            base = (plane + f) * (H + 2)
            sends_row[k][0, f * W:(f + 1) * W] = pad[base + 1, 8:8 + W].astype(BF16)
            sends_row[k][1, f * W:(f + 1) * W] = pad[base + H, 8:8 + W].astype(BF16)
            for side, column in ((0, 8), (1, 7 + W)):
                sends_col[k][side, f * H:(f + 1) * H] = flat[pl.ds((base + 1) * PITCH + column, H, stride=PITCH), :].astype(BF16)
        for d, (dr, dc) in enumerate(DIRS):
            @pl.when(exists(dr, dc))
            def _():
                rim_copy(k, d).start()

    def take_rims(k, pad, plane, count):
        for d, (dr, dc) in enumerate(DIRS):
            @pl.when(exists(-dr, -dc))
            def _():
                rim_copy(k, d).wait_recv()
        flat = pad.reshape(pad.shape[0] * PITCH, C)
        rows, cols = recvs_row[k], recvs_col[k]
        for f in range(count):
            base = (plane + f) * (H + 2)
            pad[base, 8:8 + W] = rows[1, f * W:(f + 1) * W].astype(F32)
            pad[base + H + 1, 8:8 + W] = rows[0, f * W:(f + 1) * W].astype(F32)
            for low, mid, high, column in ((0, 1, 2, 8 + W), (3, 4, 5, 7)):
                flat[pl.ds((base + 1) * PITCH + column, H, stride=PITCH), :] = cols[mid, f * H:(f + 1) * H].astype(F32)
                pad[base, column:column + 1] = cols[high, f * H:(f + 1) * H].astype(F32)[H - 1:H]
                pad[base + H + 1, column:column + 1] = cols[low, f * H:(f + 1) * H].astype(F32)[0:1]

    def stack(pad, s, plane, pad_plane):
        def step(i, _):
            for j in range(6):
                h = i * 6 + j
                row = pad_plane * (H + 2) + h
                for k in range(3):
                    s[plane, h, :, k * C:(k + 1) * C] = pad[row, 7 + k:7 + k + W].astype(BF16)
            return 0
        lax.fori_loop(0, (H + 2) // 6, step, 0)

    def taps(s, plane, w, first, last, h0=0, rows=H):
        lhs = jnp.concatenate([s[plane, h0 + k:h0 + k + rows].reshape(rows * W, 3 * C) for k in range(3)], axis=1)
        return jnp.dot(lhs, w[:, first * C:(last + 1) * C], preferred_element_type=F32)

    g1, g2 = g1_ref[...], g2_ref[...]

    copies[0].wait()
    for f in range(T):
        activate(lambda h: x_ref[f, h], g1, pad1, 2 + f)
    send_rims(0, pad1, 2, T)
    take_rims(0, pad1, 2, T)
    for f in range(T):
        stack(pad1, s1, 2 + f, 2 + f)
    for c in copies[1:4]:
        c.wait()

    for h0 in (0, H // 2):
        rows = H // 2
        mid = taps(s1, 3, w1, 1, 2, h0, rows) + taps(s1, 4, w1, 0, 1, h0, rows)
        at_rows = slice(h0 * W, (h0 + rows) * W)
        acc1[2, at_rows] = (mid[:, :C] + taps(s1, 2, w1, 2, 2, h0, rows)).astype(BF16).astype(F32)
        acc1[3, at_rows] = (mid[:, C:] + taps(s1, 5, w1, 0, 0, h0, rows)).astype(BF16).astype(F32)

    def hidden(f):
        return lambda h: acc1[f, pl.ds(pl.multiple_of(h * W, W), W)]

    for f in (2, 3):
        activate(hidden(f), g2, pad2, f)
    send_rims(1, pad2, 2, 2)

    part = taps(s1, 2, w1, 0, 1)
    acc1[0] = part[:, :C]
    acc1[1] = part[:, C:] + taps(s1, 3, w1, 0, 0)

    take_rims(1, pad2, 2, 2)
    for f in (2, 3):
        stack(pad2, s2, f, f)
    for c in copies[4:]:
        c.wait()

    late = taps(s2, 3, w2, 1, 2)
    q_out[0] = (late[:, :C] + taps(s2, 2, w2, 2, 2)).astype(BF16)
    q_out[1] = late[:, C:].astype(BF16)

    @pl.when(has_next)
    def _():
        sum_copy.start()

    part = taps(s2, 2, w2, 0, 1)
    acc2[2] = part[:, :C]
    acc2[3] = part[:, C:] + taps(s2, 3, w2, 0, 0)

    @pl.when(has_prev)
    def _():
        raw_copy.wait_recv()
    for f in range(2):
        activate(lambda h: prev_raw[f, h], g1, pad1, f)
    send_rims(2, pad1, 0, 2)
    take_rims(2, pad1, 0, 2)
    for f in range(2):
        stack(pad1, s1, f, f)

    part = taps(s1, 1, w1, 1, 2)
    acc1[0] = (acc1[0] + part[:, :C] + taps(s1, 0, w1, 2, 2)).astype(BF16).astype(F32)
    acc1[1] = (acc1[1] + part[:, C:]).astype(BF16).astype(F32)
    for f in range(2):
        activate(hidden(f), g2, pad2, f)
    send_rims(3, pad2, 0, 2)
    take_rims(3, pad2, 0, 2)
    for f in range(2):
        stack(pad2, s2, f, f)

    zero = taps(s2, 0, w2, 0, 2)
    one = taps(s2, 1, w2, 0, 2)

    def finish(f, total):
        o_ref[f] = (x_ref[f].reshape(H * W, C).astype(F32) + total).astype(BF16).reshape(H, W, C)

    finish(2, acc2[2] + zero[:, 2 * C:] + one[:, C:2 * C])
    finish(3, acc2[3] + one[:, 2 * C:])
    acc2[0] = zero[:, :C]
    acc2[1] = zero[:, C:2 * C] + one[:, :C]

    @pl.when(has_prev)
    def _():
        sum_copy.wait_recv()
    finish(0, acc2[0] + q_in[0].astype(F32))
    finish(1, acc2[1] + q_in[1].astype(F32))

    @pl.when(has_next)
    def _():
        raw_copy.wait_send()
        sum_copy.wait_send()
    for k in range(4):
        for d, (dr, dc) in enumerate(DIRS):
            @pl.when(exists(dr, dc))
            def _():
                rim_copy(k, d).wait_send()


def block(sizes, frames, gain_first, weight_first, gain_second, weight_second):
    T, H, W, C = frames.shape
    vmem = pl.BlockSpec(memory_space=pltpu.VMEM)
    hbm = pl.BlockSpec(memory_space=pl.ANY)
    counts = (T, 2, 2, 2)
    return pl.pallas_call(
        functools.partial(kernel, sizes, T, H, W, C),
        out_shape=jax.ShapeDtypeStruct(frames.shape, frames.dtype),
        in_specs=[hbm, vmem, hbm, vmem, hbm],
        out_specs=vmem,
        scratch_shapes=[
            pltpu.VMEM((T, H, W, C), BF16),
            pltpu.VMEM((9 * C, 3 * C), BF16),
            pltpu.VMEM((9 * C, 3 * C), BF16),
            pltpu.VMEM(((T + 2) * (H + 2), PITCH, C), F32),
            pltpu.VMEM((T * (H + 2), PITCH, C), F32),
            pltpu.VMEM((T + 2, H + 2, W, 3 * C), BF16),
            pltpu.VMEM((T, H + 2, W, 3 * C), BF16),
            pltpu.VMEM((T, H * W, C), F32),
            pltpu.VMEM((T, H * W, C), F32),
            pltpu.VMEM((2, H, W, C), BF16),
            pltpu.VMEM((2, H * W, C), BF16),
            pltpu.VMEM((2, H * W, C), BF16),
        ]
        + [pltpu.VMEM((2, n * W, C), BF16) for n in counts]
        + [pltpu.VMEM((2, n * H, C), BF16) for n in counts]
        + [pltpu.VMEM((2, n * W, C), BF16) for n in counts]
        + [pltpu.VMEM((6, n * H, C), BF16) for n in counts]
        + [
            pltpu.SemaphoreType.DMA((7,)),
            pltpu.SemaphoreType.DMA((2,)),
            pltpu.SemaphoreType.DMA((2,)),
            pltpu.SemaphoreType.DMA((4, len(DIRS))),
            pltpu.SemaphoreType.DMA((4, len(DIRS))),
        ],
        compiler_params=pltpu.CompilerParams(collective_id=0, has_side_effects=True, vmem_limit_bytes=60 * 2**20),
    )(
        frames,
        gain_first.reshape(1, C),
        weight_first.reshape(3, 9 * C, C),
        gain_second.reshape(1, C),
        weight_second.reshape(3, 9 * C, C),
    )


def solution(mesh):
    sizes = dict(mesh.shape)
    return jax.shard_map(
        functools.partial(block, sizes),
        mesh=mesh,
        in_specs=(P("tm", "row", "col", None), P(), P(), P(), P()),
        out_specs=P("tm", "row", "col", None),
        check_vma=False,
    )
```

```python
import functools

import jax
import jax.numpy as jnp
from jax import lax
from jax.experimental import pallas as pl
from jax.experimental.pallas import tpu as pltpu
from jax.sharding import PartitionSpec as P

MESH = pl.DeviceIdType.MESH
F32, BF16 = jnp.float32, jnp.bfloat16
DIRS = ((-1, 0), (1, 0), (0, -1), (0, 1), (-1, -1), (1, -1), (-1, 1), (1, 1))
LEFT = 8
PITCH = 48
SIDE = 24


def act(v, gain):
    half = v * lax.rsqrt(jnp.mean(v * v, axis=-1, keepdims=True) + 1e-6) * (0.5 * gain)
    return half + half * jnp.tanh(half)


def kernel(sizes, T, H, W, C, x_hbm, g1_hbm, w1_hbm, g2_hbm, w2_hbm, o_ref,
           x_ref, g1_ref, g2_ref, w1, w2, pad1, pad2, s1, t1, s2, acc1, acc2, prev_raw, q_out, q_in, stage,
           sr0, sr1, sc0, sc1, sk0, sk1, rr0, rr1, rc0, rc1, rk0, rk1,
           local_sem, y_send, y_recv, send_sem, recv_sem):
    at = {a: lax.axis_index(a) for a in ("tm", "row", "col")}
    sends = ((sr0, sc0, sk0), (sr1, sc1, sk1))
    recvs = ((rr0, rc0, rk0), (rr1, rc1, rk1))
    flat1 = pad1.reshape(pad1.shape[0] * PITCH, C)
    flat2 = pad2.reshape(pad2.shape[0] * PITCH, C)
    MAIN = (H + 2) * W

    def exists(dr, dc):
        r, c = at["row"] + dr, at["col"] + dc
        return (r >= 0) & (r < sizes["row"]) & (c >= 0) & (c < sizes["col"])

    def place(dr, dc):
        return {"row": at["row"] + dr, "col": at["col"] + dc}

    has_next, has_prev = at["tm"] + 1 < sizes["tm"], at["tm"] > 0

    frames_in = [pltpu.make_async_copy(x_hbm.at[f], x_ref.at[f], local_sem.at[f]) for f in range(T)]
    gains_in = [pltpu.make_async_copy(g1_hbm, g1_ref, local_sem.at[T]), pltpu.make_async_copy(g2_hbm, g2_ref, local_sem.at[T + 1])]
    weights_in = [
        pltpu.make_async_copy(src.at[kt], dst.at[:, (2 - kt) * C:(3 - kt) * C], local_sem.at[T + 2 + 3 * k + kt])
        for k, (src, dst) in enumerate(((w1_hbm, w1), (w2_hbm, w2))) for kt in range(3)
    ]
    for c in gains_in + frames_in + weights_in:
        c.start()

    for ref in recvs[0] + recvs[1] + (prev_raw, q_in, stage):
        ref[...] = jnp.zeros_like(ref)

    barrier = pltpu.get_barrier_semaphore()
    expected = has_next.astype(jnp.int32)

    @pl.when(has_prev)
    def _():
        pl.semaphore_signal(barrier, inc=1, device_id={"tm": at["tm"] - 1}, device_id_type=MESH)

    for dr, dc in DIRS:
        @pl.when(exists(dr, dc))
        def _():
            pl.semaphore_signal(barrier, inc=1, device_id=place(dr, dc), device_id_type=MESH)
        expected = expected + exists(dr, dc).astype(jnp.int32)
    pl.semaphore_wait(barrier, expected)

    def y_copy(src, dst, k):
        return pltpu.make_async_remote_copy(
            src_ref=src, dst_ref=dst, send_sem=y_send.at[k], recv_sem=y_recv.at[k],
            device_id={"tm": at["tm"] + 1}, device_id_type=MESH)

    raw_copy = y_copy(x_hbm.at[T - 2:T], prev_raw, 0)
    sum_copies = [y_copy(q_out.at[k], q_in.at[k], 1 + k) for k in range(2)]

    @pl.when(has_next)
    def _():
        raw_copy.start()

    def rim_copy(k, d):
        kind, index = ((0, d), (1, d - 2), (2, d - 4))[(d >= 2) + (d >= 4)]
        return pltpu.make_async_remote_copy(
            src_ref=sends[k][kind].at[index], dst_ref=recvs[k][kind].at[index],
            send_sem=send_sem.at[k, d], recv_sem=recv_sem.at[k, d],
            device_id=place(*DIRS[d]), device_id_type=MESH)

    def send_rims(k, plane, count):
        rows, cols, corners = sends[k]
        for f in range(count):
            base = (plane + f) * (H + 4) + 2
            for rr in range(2):
                for side, first in ((0, 0), (1, H - 2)):
                    rows[side, (2 * f + rr) * W:(2 * f + rr + 1) * W] = pad1[base + first + rr, LEFT:LEFT + W].astype(BF16)
                for d, top, column in ((0, 0, LEFT), (1, H - 2, LEFT), (2, 0, LEFT + W - 2), (3, H - 2, LEFT + W - 2)):
                    stage[d, 4 * f + 2 * rr:4 * f + 2 * rr + 2] = pad1[base + top + rr, column:column + 2]
            for cc in range(2):
                for side, first in ((0, LEFT), (1, LEFT + W - 2)):
                    cols[side, (2 * f + cc) * H:(2 * f + cc + 1) * H] = flat1[pl.ds(base * PITCH + first + cc, H, stride=PITCH), :].astype(BF16)
        corners[...] = stage[...].astype(BF16)
        for d, (dr, dc) in enumerate(DIRS):
            @pl.when(exists(dr, dc))
            def _():
                rim_copy(k, d).start()

    def take_rims(k, plane, count):
        for d, (dr, dc) in enumerate(DIRS):
            @pl.when(exists(-dr, -dc))
            def _():
                rim_copy(k, d).wait_recv()
        rows, cols, corners = recvs[k]
        met = [corners[d].astype(F32) for d in range(4)]
        for f in range(count):
            base = (plane + f) * (H + 4)
            for rr in range(2):
                pad1[base + rr, LEFT:LEFT + W] = rows[1, (2 * f + rr) * W:(2 * f + rr + 1) * W].astype(F32)
                pad1[base + H + 2 + rr, LEFT:LEFT + W] = rows[0, (2 * f + rr) * W:(2 * f + rr + 1) * W].astype(F32)
                for d, top, column in ((3, 0, LEFT - 2), (1, 0, LEFT + W), (2, H + 2, LEFT - 2), (0, H + 2, LEFT + W)):
                    pad1[base + top + rr, column:column + 2] = met[d][4 * f + 2 * rr:4 * f + 2 * rr + 2]
            for cc in range(2):
                for side, first in ((1, LEFT - 2), (0, LEFT + W)):
                    flat1[pl.ds((base + 2) * PITCH + first + cc, H, stride=PITCH), :] = cols[side, (2 * f + cc) * H:(2 * f + cc + 1) * H].astype(F32)

    def activate(load, gain, pad, row0, count, group):
        def step(i, _):
            for j in range(group):
                h = i * group + j
                pad[row0 + h, LEFT:LEFT + W] = act(load(h).astype(F32), gain)
            return 0
        lax.fori_loop(0, count // group, step, 0)

    def stack(pad, s, plane, row0, h0, count):
        def step(i, _):
            for j in range(2):
                h = h0 + i * 2 + j
                for k in range(3):
                    s[plane, h, :, k * C:(k + 1) * C] = pad[row0 + h, LEFT - 1 + k:LEFT - 1 + k + W].astype(BF16)
            return 0
        lax.fori_loop(0, count // 2, step, 0, unroll=True)

    def stack_first(plane):
        stack(pad1, s1, plane, plane * (H + 4), 0, H + 4)
        for kh in range(3):
            for kw in range(3):
                rim = [flat1[pl.ds((plane * (H + 4) + kh) * PITCH + column + kw, SIDE, stride=PITCH), :] for column in (LEFT - 2, LEFT + W - 1)]
                t1[plane, :, (3 * kh + kw) * C:(3 * kh + kw + 1) * C] = jnp.concatenate(rim, axis=0).astype(BF16)

    def taps(s, plane, w, first, last, h0, rows, side=None):
        lhs = jnp.concatenate([s[plane, h0 + k:h0 + k + rows].reshape(rows * W, 3 * C) for k in range(3)], axis=1)
        if side is not None:
            lhs = jnp.concatenate([lhs, side[plane]], axis=0)
        return jnp.dot(lhs, w[:, first * C:(last + 1) * C], preferred_element_type=F32)

    def store_hidden(f, total, h0, rows):
        total = total.astype(BF16).astype(F32)
        acc1[f, h0 * W:(h0 + rows) * W] = total[:rows * W]
        if total.shape[0] > rows * W:
            acc1[f, MAIN:] = total[rows * W:]

    def second(f, h0, rows, side):
        base = f * (H + 2)
        activate(lambda h: acc1[f, pl.ds(pl.multiple_of((h0 + h) * W, W), W)], g2, pad2, base + h0, rows, rows // 2)
        if side:
            rim = act(acc1[f, MAIN:], g2)
            for k, column in enumerate((LEFT - 1, LEFT + W)):
                flat2[pl.ds(base * PITCH + column, H + 2, stride=PITCH), :] = rim[k * SIDE:k * SIDE + H + 2]

                @pl.when(jnp.logical_not(exists(0, 2 * k - 1)))
                def _():
                    flat2[pl.ds(base * PITCH + column, H + 2, stride=PITCH), :] = jnp.zeros((H + 2, C), F32)
        for h, dr in ((0, -1), (H + 1, 1)):
            if h0 <= h < h0 + rows:
                @pl.when(jnp.logical_not(exists(dr, 0)))
                def _():
                    pad2[base + h] = jnp.zeros((PITCH, C), F32)
        stack(pad2, s2, f, base, h0, rows)

    for c in gains_in:
        c.wait()
    g1, g2 = g1_ref[...], g2_ref[...]
    for f in range(T):
        frames_in[f].wait()
        activate(lambda h: x_ref[f, h], g1, pad1, (2 + f) * (H + 4) + 2, H, 8)
    send_rims(0, 2, T)
    take_rims(0, 2, T)
    for f in range(T):
        stack_first(2 + f)
    for c in weights_in[:3]:
        c.wait()

    half = H // 2
    for k, (h0, rows) in enumerate(((0, half + 2), (half + 2, half))):
        side = t1 if k == 0 else None
        mid = taps(s1, 3, w1, 1, 2, h0, rows, side) + taps(s1, 4, w1, 0, 1, h0, rows, side)
        store_hidden(2, mid[:, :C] + taps(s1, 2, w1, 2, 2, h0, rows, side), h0, rows)
        store_hidden(3, mid[:, C:] + taps(s1, 5, w1, 0, 0, h0, rows, side), h0, rows)
        for f in (2, 3):
            second(f, h0, rows, k == 0)
        if k == 0:
            for c in weights_in[3:]:
                c.wait()
        late = taps(s2, 3, w2, 1, 2, k * half, half)
        q_out[k, 0] = (late[:, :C] + taps(s2, 2, w2, 2, 2, k * half, half)).astype(BF16)
        q_out[k, 1] = late[:, C:].astype(BF16)

        @pl.when(has_next)
        def _():
            sum_copies[k].start()

    @pl.when(has_prev)
    def _():
        raw_copy.wait_recv()
    for f in range(2):
        activate(lambda h: prev_raw[f, h], g1, pad1, f * (H + 4) + 2, H, 8)
    send_rims(1, 0, 2)

    part = taps(s2, 2, w2, 0, 1, 0, H)
    acc2[2] = part[:, :C]
    acc2[3] = part[:, C:] + taps(s2, 3, w2, 0, 0, 0, H)
    part = taps(s1, 2, w1, 0, 1, 0, H + 2, t1)
    acc1[0] = part[:, :C]
    acc1[1] = part[:, C:] + taps(s1, 3, w1, 0, 0, 0, H + 2, t1)

    take_rims(1, 0, 2)
    for f in range(2):
        stack_first(f)

    part = taps(s1, 1, w1, 1, 2, 0, H + 2, t1)
    store_hidden(0, acc1[0] + part[:, :C] + taps(s1, 0, w1, 2, 2, 0, H + 2, t1), 0, H + 2)
    store_hidden(1, acc1[1] + part[:, C:], 0, H + 2)
    for f in range(2):
        second(f, 0, H + 2, True)

    zero = taps(s2, 0, w2, 0, 2, 0, H)
    one = taps(s2, 1, w2, 0, 2, 0, H)

    def finish(f, h0, rows, total):
        own = x_ref[f, h0:h0 + rows].reshape(rows * W, C).astype(F32)
        o_ref[f, h0:h0 + rows] = (own + total).astype(BF16).reshape(rows, W, C)

    finish(2, 0, H, acc2[2] + zero[:, 2 * C:] + one[:, C:2 * C])
    finish(3, 0, H, acc2[3] + one[:, 2 * C:])
    acc2[0] = zero[:, :C]
    acc2[1] = zero[:, C:2 * C] + one[:, :C]

    for k in range(2):
        @pl.when(has_prev)
        def _():
            sum_copies[k].wait_recv()
        for f in range(2):
            finish(f, k * half, half, acc2[f, k * half * W:(k + 1) * half * W] + q_in[k, f].astype(F32))

    @pl.when(has_next)
    def _():
        for c in [raw_copy] + sum_copies:
            c.wait_send()
    for k in range(2):
        for d, (dr, dc) in enumerate(DIRS):
            @pl.when(exists(dr, dc))
            def _():
                rim_copy(k, d).wait_send()


def block(sizes, frames, gain_first, weight_first, gain_second, weight_second):
    T, H, W, C = frames.shape
    hbm = pl.BlockSpec(memory_space=pl.ANY)
    rims = [shape for n in (T, 2) for shape in ((2, n * 2 * W, C),)]
    cols = [shape for n in (T, 2) for shape in ((2, n * 2 * H, C),)]
    corners = [(4, 16, C)] * 2
    return pl.pallas_call(
        functools.partial(kernel, sizes, T, H, W, C),
        out_shape=pltpu.VMEM(frames.shape, frames.dtype),
        in_specs=[hbm] * 5,
        out_specs=pl.BlockSpec(memory_space=pltpu.VMEM),
        scratch_shapes=[
            pltpu.VMEM((T, H, W, C), BF16),
            pltpu.VMEM((1, C), F32),
            pltpu.VMEM((1, C), F32),
            pltpu.VMEM((9 * C, 3 * C), BF16),
            pltpu.VMEM((9 * C, 3 * C), BF16),
            pltpu.VMEM(((T + 2) * (H + 4) + 8, PITCH, C), F32),
            pltpu.VMEM((T * (H + 2), PITCH, C), F32),
            pltpu.VMEM((T + 2, H + 4, W, 3 * C), BF16),
            pltpu.VMEM((T + 2, 2 * SIDE, 9 * C), BF16),
            pltpu.VMEM((T, H + 2, W, 3 * C), BF16),
            pltpu.VMEM((T, (H + 2) * W + 2 * SIDE, C), F32),
            pltpu.VMEM((T, H * W, C), F32),
            pltpu.VMEM((2, H, W, C), BF16),
            pltpu.VMEM((2, 2, H * W // 2, C), BF16),
            pltpu.VMEM((2, 2, H * W // 2, C), BF16),
            pltpu.VMEM((4, 16, C), F32),
        ]
        + [pltpu.VMEM(shape, BF16) for shape in (rims + cols + corners) * 2]
        + [
            pltpu.SemaphoreType.DMA((T + 8,)),
            pltpu.SemaphoreType.DMA((3,)),
            pltpu.SemaphoreType.DMA((3,)),
            pltpu.SemaphoreType.DMA((2, len(DIRS))),
            pltpu.SemaphoreType.DMA((2, len(DIRS))),
        ],
        compiler_params=pltpu.CompilerParams(collective_id=0, has_side_effects=True, vmem_limit_bytes=60 * 2**20),
    )(
        frames,
        gain_first.reshape(1, C),
        weight_first.reshape(3, 9 * C, C),
        gain_second.reshape(1, C),
        weight_second.reshape(3, 9 * C, C),
    )


def solution(mesh):
    sizes = dict(mesh.shape)
    return jax.shard_map(
        functools.partial(block, sizes),
        mesh=mesh,
        in_specs=(P("tm", "row", "col", None), P(), P(), P(), P()),
        out_specs=P("tm", "row", "col", None),
        check_vma=False,
    )
```

```python
import functools

import jax
import jax.numpy as jnp
from jax import lax
from jax.experimental import pallas as pl
from jax.experimental.pallas import tpu as pltpu
from jax.sharding import PartitionSpec as P

MESH = pl.DeviceIdType.MESH
F32, BF16 = jnp.float32, jnp.bfloat16
DIRS = ((-1, 0), (1, 0), (0, -1), (0, 1), (-1, -1), (1, -1), (-1, 1), (1, 1))
LEFT = 8
PITCH = 48
SIDE = 24
BARRIER_AT = 3


def act(v, gain):
    half = v * lax.rsqrt(jnp.mean(v * v, axis=-1, keepdims=True) + 1e-6) * (0.5 * gain)
    return half + half * jnp.tanh(half)


def kernel(sizes, T, H, W, C, x_hbm, g1_hbm, w1_hbm, g2_hbm, w2_hbm, o_ref,
           x_ref, g1_ref, g2_ref, w1, w2, pad1, pad2, s1, t1, s2, acc1, acc2, prev_raw, q_out, q_in, stage,
           sr0, sr1, sc0, sc1, sk0, sk1, rr0, rr1, rc0, rc1, rk0, rk1,
           local_sem, y_send, y_recv, send_sem, recv_sem):
    at = {a: lax.axis_index(a) for a in ("tm", "row", "col")}
    sends = ((sr0, sc0, sk0), (sr1, sc1, sk1))
    recvs = ((rr0, rc0, rk0), (rr1, rc1, rk1))
    flat1 = pad1.reshape(pad1.shape[0] * PITCH, C)
    flat2 = pad2.reshape(pad2.shape[0] * PITCH, C)
    MAIN = (H + 2) * W
    COLUMNS = (-1, 0, W - 1, W)
    INNER = ((2, H - 2),)
    OUTER = ((0, 2), (H, 2))

    def exists(dr, dc):
        r, c = at["row"] + dr, at["col"] + dc
        return (r >= 0) & (r < sizes["row"]) & (c >= 0) & (c < sizes["col"])

    def place(dr, dc):
        return {"row": at["row"] + dr, "col": at["col"] + dc}

    has_next, has_prev = at["tm"] + 1 < sizes["tm"], at["tm"] > 0

    frames_in = [pltpu.make_async_copy(x_hbm.at[f], x_ref.at[f], local_sem.at[f]) for f in range(T)]
    gains_in = [pltpu.make_async_copy(g1_hbm, g1_ref, local_sem.at[T]), pltpu.make_async_copy(g2_hbm, g2_ref, local_sem.at[T + 1])]
    weights_in = [
        pltpu.make_async_copy(src.at[kt], dst.at[:, (2 - kt) * C:(3 - kt) * C], local_sem.at[T + 2 + 3 * k + kt])
        for k, (src, dst) in enumerate(((w1_hbm, w1), (w2_hbm, w2))) for kt in range(3)
    ]
    for c in gains_in + frames_in + weights_in:
        c.start()

    for ref in recvs[0] + recvs[1] + (prev_raw, q_in, stage):
        ref[...] = jnp.zeros_like(ref)

    barrier = pltpu.get_barrier_semaphore()
    expected = has_next.astype(jnp.int32)

    @pl.when(has_prev)
    def _():
        pl.semaphore_signal(barrier, inc=1, device_id={"tm": at["tm"] - 1}, device_id_type=MESH)

    for dr, dc in DIRS:
        @pl.when(exists(dr, dc))
        def _():
            pl.semaphore_signal(barrier, inc=1, device_id=place(dr, dc), device_id_type=MESH)
        expected = expected + exists(dr, dc).astype(jnp.int32)
    def y_copy(src, dst, k):
        return pltpu.make_async_remote_copy(
            src_ref=src, dst_ref=dst, send_sem=y_send.at[k], recv_sem=y_recv.at[k],
            device_id={"tm": at["tm"] + 1}, device_id_type=MESH)

    raw_copy = y_copy(x_hbm.at[T - 2:T], prev_raw, 0)
    sum_copies = [y_copy(q_out.at[k], q_in.at[k], 1 + k) for k in range(2)]

    def rim_copy(k, d):
        kind, index = ((0, d), (1, d - 2), (2, d - 4))[(d >= 2) + (d >= 4)]
        return pltpu.make_async_remote_copy(
            src_ref=sends[k][kind].at[index], dst_ref=recvs[k][kind].at[index],
            send_sem=send_sem.at[k, d], recv_sem=recv_sem.at[k, d],
            device_id=place(*DIRS[d]), device_id_type=MESH)

    def send_rims(k, plane, count):
        rows, cols, corners = sends[k]
        for f in range(count):
            base = (plane + f) * (H + 4) + 2
            for rr in range(2):
                for side, first in ((0, 0), (1, H - 2)):
                    rows[side, (2 * f + rr) * W:(2 * f + rr + 1) * W] = pad1[base + first + rr, LEFT:LEFT + W].astype(BF16)
                for d, top, column in ((0, 0, LEFT), (1, H - 2, LEFT), (2, 0, LEFT + W - 2), (3, H - 2, LEFT + W - 2)):
                    stage[d, 4 * f + 2 * rr:4 * f + 2 * rr + 2] = pad1[base + top + rr, column:column + 2]
            for cc in range(2):
                for side, first in ((0, LEFT), (1, LEFT + W - 2)):
                    cols[side, (2 * f + cc) * H:(2 * f + cc + 1) * H] = flat1[pl.ds(base * PITCH + first + cc, H, stride=PITCH), :].astype(BF16)
        corners[...] = stage[...].astype(BF16)
        for d, (dr, dc) in enumerate(DIRS):
            @pl.when(exists(dr, dc))
            def _():
                rim_copy(k, d).start()

    def take_rims(k, plane, count):
        for d, (dr, dc) in enumerate(DIRS):
            @pl.when(exists(-dr, -dc))
            def _():
                rim_copy(k, d).wait_recv()
        rows, cols, corners = recvs[k]
        met = [corners[d].astype(F32) for d in range(4)]
        for f in range(count):
            base = (plane + f) * (H + 4)
            for rr in range(2):
                pad1[base + rr, LEFT:LEFT + W] = rows[1, (2 * f + rr) * W:(2 * f + rr + 1) * W].astype(F32)
                pad1[base + H + 2 + rr, LEFT:LEFT + W] = rows[0, (2 * f + rr) * W:(2 * f + rr + 1) * W].astype(F32)
                for d, top, column in ((3, 0, LEFT - 2), (1, 0, LEFT + W), (2, H + 2, LEFT - 2), (0, H + 2, LEFT + W)):
                    pad1[base + top + rr, column:column + 2] = met[d][4 * f + 2 * rr:4 * f + 2 * rr + 2]
            for cc in range(2):
                for side, first in ((1, LEFT - 2), (0, LEFT + W)):
                    flat1[pl.ds((base + 2) * PITCH + first + cc, H, stride=PITCH), :] = cols[side, (2 * f + cc) * H:(2 * f + cc + 1) * H].astype(F32)

    def activate(load, gain, pad, row0, count, group):
        def step(i, _):
            for j in range(group):
                h = i * group + j
                pad[row0 + h, LEFT:LEFT + W] = act(load(h).astype(F32), gain)
            return 0
        lax.fori_loop(0, count // group, step, 0)

    def stack(pad, s, plane, row0, h0, count):
        def step(i, _):
            for j in range(2):
                h = h0 + i * 2 + j
                for k in range(3):
                    s[plane, h, :, k * C:(k + 1) * C] = pad[row0 + h, LEFT - 1 + k:LEFT - 1 + k + W].astype(BF16)
            return 0
        lax.fori_loop(0, count // 2, step, 0, unroll=True)

    def stack_inner(plane):
        stack(pad1, s1, plane, plane * (H + 4), 2, H)

    def stack_outer(plane):
        for h0 in (0, H + 2):
            stack(pad1, s1, plane, plane * (H + 4), h0, 2)
        for kh in range(3):
            for kw in range(3):
                rim = [flat1[pl.ds((plane * (H + 4) + kh) * PITCH + LEFT - 1 + column + kw, SIDE, stride=PITCH), :] for column in COLUMNS]
                t1[plane, :, (3 * kh + kw) * C:(3 * kh + kw + 1) * C] = jnp.concatenate(rim, axis=0).astype(BF16)

    def taps(s, plane, w, first, last, parts, side=None):
        lhs = [jnp.concatenate([s[plane, h0 + k:h0 + k + rows].reshape(rows * W, 3 * C) for k in range(3)], axis=1) for h0, rows in parts]
        if side is not None:
            lhs.append(side[plane])
        return jnp.dot(jnp.concatenate(lhs, axis=0), w[:, first * C:(last + 1) * C], preferred_element_type=F32)

    def places(parts):
        n = 0
        for h0, rows in parts:
            yield slice(h0 * W, (h0 + rows) * W), slice(n, n + rows * W)
            n += rows * W
        if parts is OUTER:
            yield slice(MAIN, MAIN + len(COLUMNS) * SIDE), slice(n, n + len(COLUMNS) * SIDE)

    def store_hidden(f, total, parts, final, add=False):
        for dst, src in places(parts):
            value = total[src]
            if add:
                value = value + acc1[f, dst]
            acc1[f, dst] = value.astype(BF16).astype(F32) if final else value

    def second_inner(f):
        activate(lambda h: acc1[f, pl.ds(pl.multiple_of((2 + h) * W, W), W)], g2, pad2, f * (H + 2) + 2, H - 2, (H - 2) // 2)

    def second_outer(f):
        base = f * (H + 2)
        for h0, rows in OUTER:
            for h in range(h0, h0 + rows):
                pad2[base + h, LEFT:LEFT + W] = act(acc1[f, h * W:(h + 1) * W], g2)
        rim = act(acc1[f, MAIN:], g2)
        for k, column in enumerate(COLUMNS):
            flat2[pl.ds(base * PITCH + LEFT + column, H + 2, stride=PITCH), :] = rim[k * SIDE:k * SIDE + H + 2]
        for column, dc in ((-1, -1), (W, 1)):
            @pl.when(jnp.logical_not(exists(0, dc)))
            def _():
                flat2[pl.ds(base * PITCH + LEFT + column, H + 2, stride=PITCH), :] = jnp.zeros((H + 2, C), F32)
        for h, dr in ((0, -1), (H + 1, 1)):
            @pl.when(jnp.logical_not(exists(dr, 0)))
            def _():
                pad2[base + h] = jnp.zeros((PITCH, C), F32)
        stack(pad2, s2, f, base, 0, H + 2)

    def early_hidden(parts, side):
        mid = taps(s1, 3, w1, 1, 2, parts, side) + taps(s1, 4, w1, 0, 1, parts, side)
        store_hidden(2, mid[:, :C] + taps(s1, 2, w1, 2, 2, parts, side), parts, True)
        store_hidden(3, mid[:, C:] + taps(s1, 5, w1, 0, 0, parts, side), parts, True)

    def early_share(parts, side):
        part = taps(s1, 2, w1, 0, 1, parts, side)
        store_hidden(0, part[:, :C], parts, False)
        store_hidden(1, part[:, C:] + taps(s1, 3, w1, 0, 0, parts, side), parts, False)

    def late_hidden(parts, side):
        part = taps(s1, 1, w1, 1, 2, parts, side)
        store_hidden(0, part[:, :C] + taps(s1, 0, w1, 2, 2, parts, side), parts, True, True)
        store_hidden(1, part[:, C:], parts, True, True)

    for c in gains_in:
        c.wait()
    g1, g2 = g1_ref[...], g2_ref[...]
    for f in range(T):
        frames_in[f].wait()
        activate(lambda h: x_ref[f, h], g1, pad1, (2 + f) * (H + 4) + 2, H, 8)
        if f == BARRIER_AT:
            pl.semaphore_wait(barrier, expected)

            @pl.when(has_next)
            def _():
                raw_copy.start()
    send_rims(0, 2, T)

    for f in range(T):
        stack_inner(2 + f)
    for c in weights_in[:3]:
        c.wait()
    early_hidden(INNER, None)
    for f in (2, 3):
        second_inner(f)
    early_share(INNER, None)

    take_rims(0, 2, T)
    for f in range(T):
        stack_outer(2 + f)
    early_hidden(OUTER, t1)
    for f in (2, 3):
        second_outer(f)

    for c in weights_in[3:]:
        c.wait()
    half = H // 2
    for k in range(2):
        rows = ((k * half, half),)
        late = taps(s2, 3, w2, 1, 2, rows)
        q_out[k, 0] = (late[:, :C] + taps(s2, 2, w2, 2, 2, rows)).astype(BF16)
        q_out[k, 1] = late[:, C:].astype(BF16)

        @pl.when(has_next)
        def _():
            sum_copies[k].start()
    early_share(OUTER, t1)
    whole = ((0, H),)

    @pl.when(has_prev)
    def _():
        raw_copy.wait_recv()
    for f in range(2):
        activate(lambda h: prev_raw[f, h], g1, pad1, f * (H + 4) + 2, H, 8)
    send_rims(1, 0, 2)

    for f in range(2):
        stack_inner(f)
    late_hidden(INNER, None)
    for f in range(2):
        second_inner(f)
    part = taps(s2, 2, w2, 0, 1, whole)
    acc2[2] = part[:, :C]
    acc2[3] = part[:, C:] + taps(s2, 3, w2, 0, 0, whole)

    take_rims(1, 0, 2)
    for f in range(2):
        stack_outer(f)
    late_hidden(OUTER, t1)
    for f in range(2):
        second_outer(f)

    zero = taps(s2, 0, w2, 0, 2, whole)
    one = taps(s2, 1, w2, 0, 2, whole)

    def finish(f, h0, rows, total):
        own = x_ref[f, h0:h0 + rows].reshape(rows * W, C).astype(F32)
        o_ref[f, h0:h0 + rows] = (own + total).astype(BF16).reshape(rows, W, C)

    finish(2, 0, H, acc2[2] + zero[:, 2 * C:] + one[:, C:2 * C])
    finish(3, 0, H, acc2[3] + one[:, 2 * C:])
    acc2[0] = zero[:, :C]
    acc2[1] = zero[:, C:2 * C] + one[:, :C]

    for k in range(2):
        @pl.when(has_prev)
        def _():
            sum_copies[k].wait_recv()
        for f in range(2):
            finish(f, k * half, half, acc2[f, k * half * W:(k + 1) * half * W] + q_in[k, f].astype(F32))

    @pl.when(has_next)
    def _():
        for c in [raw_copy] + sum_copies:
            c.wait_send()
    for k in range(2):
        for d, (dr, dc) in enumerate(DIRS):
            @pl.when(exists(dr, dc))
            def _():
                rim_copy(k, d).wait_send()


def block(sizes, frames, gain_first, weight_first, gain_second, weight_second):
    T, H, W, C = frames.shape
    hbm = pl.BlockSpec(memory_space=pl.ANY)
    rims = [shape for n in (T, 2) for shape in ((2, n * 2 * W, C),)]
    cols = [shape for n in (T, 2) for shape in ((2, n * 2 * H, C),)]
    corners = [(4, 16, C)] * 2
    return pl.pallas_call(
        functools.partial(kernel, sizes, T, H, W, C),
        out_shape=pltpu.VMEM(frames.shape, frames.dtype),
        in_specs=[hbm] * 5,
        out_specs=pl.BlockSpec(memory_space=pltpu.VMEM),
        scratch_shapes=[
            pltpu.VMEM((T, H, W, C), BF16),
            pltpu.VMEM((1, C), F32),
            pltpu.VMEM((1, C), F32),
            pltpu.VMEM((9 * C, 3 * C), BF16),
            pltpu.VMEM((9 * C, 3 * C), BF16),
            pltpu.VMEM(((T + 2) * (H + 4) + 8, PITCH, C), F32),
            pltpu.VMEM((T * (H + 2), PITCH, C), F32),
            pltpu.VMEM((T + 2, H + 4, W, 3 * C), BF16),
            pltpu.VMEM((T + 2, 4 * SIDE, 9 * C), BF16),
            pltpu.VMEM((T, H + 2, W, 3 * C), BF16),
            pltpu.VMEM((T, (H + 2) * W + 4 * SIDE, C), F32),
            pltpu.VMEM((T, H * W, C), F32),
            pltpu.VMEM((2, H, W, C), BF16),
            pltpu.VMEM((2, 2, H * W // 2, C), BF16),
            pltpu.VMEM((2, 2, H * W // 2, C), BF16),
            pltpu.VMEM((4, 16, C), F32),
        ]
        + [pltpu.VMEM(shape, BF16) for shape in (rims + cols + corners) * 2]
        + [
            pltpu.SemaphoreType.DMA((T + 8,)),
            pltpu.SemaphoreType.DMA((3,)),
            pltpu.SemaphoreType.DMA((3,)),
            pltpu.SemaphoreType.DMA((2, len(DIRS))),
            pltpu.SemaphoreType.DMA((2, len(DIRS))),
        ],
        compiler_params=pltpu.CompilerParams(collective_id=0, has_side_effects=True, vmem_limit_bytes=60 * 2**20),
    )(
        frames,
        gain_first.reshape(1, C),
        weight_first.reshape(3, 9 * C, C),
        gain_second.reshape(1, C),
        weight_second.reshape(3, 9 * C, C),
    )


def solution(mesh):
    sizes = dict(mesh.shape)
    return jax.shard_map(
        functools.partial(block, sizes),
        mesh=mesh,
        in_specs=(P("tm", "row", "col", None), P(), P(), P(), P()),
        out_specs=P("tm", "row", "col", None),
        check_vma=False,
    )
```

```python
import functools

import jax
import jax.numpy as jnp
from jax import lax
from jax.experimental import pallas as pl
from jax.experimental.pallas import tpu as pltpu
from jax.sharding import PartitionSpec as P

MESH = pl.DeviceIdType.MESH
F32, BF16 = jnp.float32, jnp.bfloat16
DIRS = ((-1, 0), (1, 0), (0, -1), (0, 1), (-1, -1), (1, -1), (-1, 1), (1, 1))
LEFT = 8
PITCH = 48
SIDE = 24
BARRIER_AT = 0


def act(v, gain):
    half = v * lax.rsqrt(jnp.mean(v * v, axis=-1, keepdims=True) + 1e-6) * (0.5 * gain)
    return half + half * jnp.tanh(half)


def kernel(sizes, T, H, W, C, x_hbm, g1_hbm, w1_hbm, g2_hbm, w2_hbm, o_ref,
           x_ref, g1_ref, g2_ref, w1, w2, pad1, pad2, s1, t1, s2, t2, acc1, acc2, prev_raw, qi_out, qo_out, qi_in, qo_in, stage,
           sr0, sr1, sc0, sc1, sk0, sk1, rr0, rr1, rc0, rc1, rk0, rk1,
           local_sem, y_send, y_recv, send_sem, recv_sem, here_sem):
    at = {a: lax.axis_index(a) for a in ("tm", "row", "col")}
    sends = ((sr0, sc0, sk0), (sr1, sc1, sk1))
    recvs = ((rr0, rc0, rk0), (rr1, rc1, rk1))
    flat1 = pad1.reshape(pad1.shape[0] * PITCH, C)
    flat2 = pad2.reshape(pad2.shape[0] * PITCH, C)
    PLANE2 = acc2.shape[1]
    flat_acc2 = acc2.reshape(T * PLANE2, C)
    MAIN = (H + 2) * W
    COLUMNS = (-1, 0, W - 1, W)
    INNER = ((2, H - 2),)
    OUTER = ((0, 2), (H, 2))
    COLUMNS2 = (0, 1, W - 2, W - 1)
    INNER2 = ((2, H - 4),)
    OUTER2 = ((0, 2), (H - 2, 2))

    def exists(dr, dc):
        r, c = at["row"] + dr, at["col"] + dc
        return (r >= 0) & (r < sizes["row"]) & (c >= 0) & (c < sizes["col"])

    def place(dr, dc):
        return {"row": at["row"] + dr, "col": at["col"] + dc}

    has_next, has_prev = at["tm"] + 1 < sizes["tm"], at["tm"] > 0

    frames_in = [pltpu.make_async_copy(x_hbm.at[f], x_ref.at[f], local_sem.at[f]) for f in range(T)]
    gains_in = [pltpu.make_async_copy(g1_hbm, g1_ref, local_sem.at[T]), pltpu.make_async_copy(g2_hbm, g2_ref, local_sem.at[T + 1])]
    weights_in = [
        pltpu.make_async_copy(src.at[kt], dst.at[:, (2 - kt) * C:(3 - kt) * C], local_sem.at[T + 2 + 3 * k + kt])
        for k, (src, dst) in enumerate(((w1_hbm, w1), (w2_hbm, w2))) for kt in range(3)
    ]
    for c in gains_in + frames_in + weights_in:
        c.start()

    for ref in recvs[0] + recvs[1] + (prev_raw, qi_in, qo_in, stage):
        ref[...] = jnp.zeros_like(ref)

    def is_root(dr, dc):
        return (at["tm"] == 0) & (at["row"] + dr == 0) & (at["col"] + dc == 0)

    def earlier(dr, dc):
        by_place = dc > 0 or (dc == 0 and dr > 0)
        return jnp.logical_not(is_root(0, 0)) if by_place else is_root(dr, dc)

    def later(dr, dc):
        return jnp.logical_not(earlier(dr, dc))

    barrier = pltpu.get_barrier_semaphore()
    expected = has_next.astype(jnp.int32)

    @pl.when(has_prev)
    def _():
        pl.semaphore_signal(barrier, inc=1, device_id={"tm": at["tm"] - 1}, device_id_type=MESH)

    for dr, dc in DIRS:
        @pl.when(exists(dr, dc) & earlier(dr, dc))
        def _():
            pl.semaphore_signal(barrier, inc=1, device_id=place(dr, dc), device_id_type=MESH)
        expected = expected + (exists(dr, dc) & later(dr, dc)).astype(jnp.int32)
    def y_copy(src, dst, k):
        return pltpu.make_async_remote_copy(
            src_ref=src, dst_ref=dst, send_sem=y_send.at[k], recv_sem=y_recv.at[k],
            device_id={"tm": at["tm"] + 1}, device_id_type=MESH)

    raw_copy = y_copy(x_hbm.at[T - 2:T], prev_raw, 0)
    sum_copies = [y_copy(qi_out, qi_in, 1), y_copy(qo_out, qo_in, 2)]

    def rim_copy(k, d):
        kind, index = ((0, d), (1, d - 2), (2, d - 4))[(d >= 2) + (d >= 4)]
        return pltpu.make_async_remote_copy(
            src_ref=sends[k][kind].at[index], dst_ref=recvs[k][kind].at[index],
            send_sem=send_sem.at[k, d], recv_sem=recv_sem.at[k, d],
            device_id=place(*DIRS[d]), device_id_type=MESH)

    def send_rims(k, plane, count):
        rows, cols, corners = sends[k]
        for f in range(count):
            base = (plane + f) * (H + 4) + 2
            for rr in range(2):
                for side, first in ((0, 0), (1, H - 2)):
                    rows[side, (2 * f + rr) * W:(2 * f + rr + 1) * W] = pad1[base + first + rr, LEFT:LEFT + W].astype(BF16)
                for d, top, column in ((0, 0, LEFT), (1, H - 2, LEFT), (2, 0, LEFT + W - 2), (3, H - 2, LEFT + W - 2)):
                    stage[d, 4 * f + 2 * rr:4 * f + 2 * rr + 2] = pad1[base + top + rr, column:column + 2]
            for cc in range(2):
                for side, first in ((0, LEFT), (1, LEFT + W - 2)):
                    cols[side, (2 * f + cc) * H:(2 * f + cc + 1) * H] = flat1[pl.ds(base * PITCH + first + cc, H, stride=PITCH), :].astype(BF16)
        corners[...] = stage[...].astype(BF16)
        for d, (dr, dc) in enumerate(DIRS):
            @pl.when((exists(dr, dc) & later(dr, dc)) if k == 0 else (exists(dr, dc) & has_prev))
            def _():
                rim_copy(k, d).start()

    def send_first_rims_late(root):
        for d, (dr, dc) in enumerate(DIRS):
            there = is_root(dr, dc)
            @pl.when(exists(dr, dc) & earlier(dr, dc) & (there if root else jnp.logical_not(there)))
            def _():
                pl.semaphore_wait(here_sem.at[d], 1)
                rim_copy(0, d).start()

    def take_rims(k, plane, count):
        for d, (dr, dc) in enumerate(DIRS):
            @pl.when(exists(-dr, -dc) if k == 0 else (exists(-dr, -dc) & has_prev))
            def _():
                rim_copy(k, d).wait_recv()
        rows, cols, corners = recvs[k]
        met = [corners[d].astype(F32) for d in range(4)]
        for f in range(count):
            base = (plane + f) * (H + 4)
            for rr in range(2):
                pad1[base + rr, LEFT:LEFT + W] = rows[1, (2 * f + rr) * W:(2 * f + rr + 1) * W].astype(F32)
                pad1[base + H + 2 + rr, LEFT:LEFT + W] = rows[0, (2 * f + rr) * W:(2 * f + rr + 1) * W].astype(F32)
                for d, top, column in ((3, 0, LEFT - 2), (1, 0, LEFT + W), (2, H + 2, LEFT - 2), (0, H + 2, LEFT + W)):
                    pad1[base + top + rr, column:column + 2] = met[d][4 * f + 2 * rr:4 * f + 2 * rr + 2]
            for cc in range(2):
                for side, first in ((1, LEFT - 2), (0, LEFT + W)):
                    flat1[pl.ds((base + 2) * PITCH + first + cc, H, stride=PITCH), :] = cols[side, (2 * f + cc) * H:(2 * f + cc + 1) * H].astype(F32)

    def activate(load, gain, pad, row0, count):
        for h in range(count):
            pad[row0 + h, LEFT:LEFT + W] = act(load(h).astype(F32), gain)

    def stack(pad, s, plane, row0, h0, count):
        def step(i, _):
            for j in range(2):
                h = h0 + i * 2 + j
                for k in range(3):
                    s[plane, h, :, k * C:(k + 1) * C] = pad[row0 + h, LEFT - 1 + k:LEFT - 1 + k + W].astype(BF16)
            return 0
        lax.fori_loop(0, count // 2, step, 0, unroll=True)

    def stack_inner(plane):
        stack(pad1, s1, plane, plane * (H + 4), 2, H)

    def stack_outer(plane):
        for h0 in (0, H + 2):
            stack(pad1, s1, plane, plane * (H + 4), h0, 2)
        for kh in range(3):
            for kw in range(3):
                rim = [flat1[pl.ds((plane * (H + 4) + kh) * PITCH + LEFT - 1 + column + kw, SIDE, stride=PITCH), :] for column in COLUMNS]
                t1[plane, :, (3 * kh + kw) * C:(3 * kh + kw + 1) * C] = jnp.concatenate(rim, axis=0).astype(BF16)

    def taps(s, plane, w, first, last, parts, side=None):
        lhs = [jnp.concatenate([s[plane, h0 + k:h0 + k + rows].reshape(rows * W, 3 * C) for k in range(3)], axis=1) for h0, rows in parts]
        if side is not None:
            lhs.append(side[plane])
        return jnp.dot(jnp.concatenate(lhs, axis=0), w[:, first * C:(last + 1) * C], preferred_element_type=F32)

    def places(parts):
        n = 0
        for h0, rows in parts:
            yield slice(h0 * W, (h0 + rows) * W), slice(n, n + rows * W)
            n += rows * W
        if parts is OUTER:
            yield slice(MAIN, MAIN + len(COLUMNS) * SIDE), slice(n, n + len(COLUMNS) * SIDE)
        if parts is OUTER2:
            yield slice(H * W, H * W + len(COLUMNS2) * H), slice(n, n + len(COLUMNS2) * H)

    def store_hidden(f, total, parts, final, add=False):
        for dst, src in places(parts):
            value = total[src]
            if add:
                value = value + acc1[f, dst]
            acc1[f, dst] = value.astype(BF16).astype(F32) if final else value

    def second_inner(f):
        activate(lambda h: acc1[f, (2 + h) * W:(3 + h) * W], g2, pad2, f * (H + 2) + 2, H - 2)
        stack(pad2, s2, f, f * (H + 2), 2, H - 2)

    def second_outer(f):
        base = f * (H + 2)
        for h0, rows in OUTER:
            for h in range(h0, h0 + rows):
                pad2[base + h, LEFT:LEFT + W] = act(acc1[f, h * W:(h + 1) * W], g2)
        rim = act(acc1[f, MAIN:], g2)
        for k, column in enumerate(COLUMNS):
            flat2[pl.ds(base * PITCH + LEFT + column, H + 2, stride=PITCH), :] = rim[k * SIDE:k * SIDE + H + 2]
        for column, dc in ((-1, -1), (W, 1)):
            @pl.when(jnp.logical_not(exists(0, dc)))
            def _():
                flat2[pl.ds(base * PITCH + LEFT + column, H + 2, stride=PITCH), :] = jnp.zeros((H + 2, C), F32)
        for h, dr in ((0, -1), (H + 1, 1)):
            @pl.when(jnp.logical_not(exists(dr, 0)))
            def _():
                pad2[base + h] = jnp.zeros((PITCH, C), F32)
        for h0 in (0, H - 2):
            stack(pad2, s2, f, base, h0, 4)
        for kh in range(3):
            for kw in range(3):
                rim = [flat2[pl.ds((base + kh) * PITCH + LEFT - 1 + column + kw, H, stride=PITCH), :] for column in COLUMNS2]
                t2[f, :, (3 * kh + kw) * C:(3 * kh + kw + 1) * C] = jnp.concatenate(rim, axis=0).astype(BF16)

    def early_hidden(parts, side):
        mid = taps(s1, 3, w1, 1, 2, parts, side) + taps(s1, 4, w1, 0, 1, parts, side)
        store_hidden(2, mid[:, :C] + taps(s1, 2, w1, 2, 2, parts, side), parts, True)
        store_hidden(3, mid[:, C:] + taps(s1, 5, w1, 0, 0, parts, side), parts, True)

    def early_share(parts, side):
        part = taps(s1, 2, w1, 0, 1, parts, side)
        store_hidden(0, part[:, :C], parts, False)
        store_hidden(1, part[:, C:] + taps(s1, 3, w1, 0, 0, parts, side), parts, False)

    def late_hidden(parts, side):
        part = taps(s1, 1, w1, 1, 2, parts, side)
        store_hidden(0, part[:, :C] + taps(s1, 0, w1, 2, 2, parts, side), parts, True, True)
        store_hidden(1, part[:, C:], parts, True, True)

    for c in gains_in:
        c.wait()
    g1, g2 = g1_ref[...], g2_ref[...]
    for f in range(T):
        frames_in[f].wait()
        activate(lambda h: x_ref[f, h], g1, pad1, (2 + f) * (H + 4) + 2, H)
        if f == BARRIER_AT:
            @pl.when(expected > 0)
            def _():
                pl.semaphore_wait(barrier, expected)

            @pl.when(has_next)
            def _():
                raw_copy.start()

            for d, (dr, dc) in enumerate(DIRS):
                @pl.when(exists(dr, dc) & later(dr, dc))
                def _():
                    pl.semaphore_signal(here_sem.at[DIRS.index((-dr, -dc))], inc=1, device_id=place(dr, dc), device_id_type=MESH)
    send_rims(0, 2, T)

    def make_sums(parts, side, out):
        late = taps(s2, 3, w2, 1, 2, parts, side)
        out[0] = (late[:, :C] + taps(s2, 2, w2, 2, 2, parts, side)).astype(BF16)
        out[1] = late[:, C:].astype(BF16)

    def start_sums(copy):
        @pl.when(has_next)
        def _():
            copy.start()

    def own_share(parts, side):
        part = taps(s2, 2, w2, 0, 1, parts, side)
        other = taps(s2, 3, w2, 0, 0, parts, side)
        for dst, src in places(parts):
            acc2[2, dst] = part[src, :C]
            acc2[3, dst] = part[src, C:] + other[src]

    def late_share(parts, side):
        zero = taps(s2, 0, w2, 0, 2, parts, side)
        one = taps(s2, 1, w2, 0, 2, parts, side)
        for dst, src in places(parts):
            acc2[0, dst] = zero[src, :C]
            acc2[1, dst] = zero[src, C:2 * C] + one[src, :C]
            acc2[2, dst] += zero[src, 2 * C:] + one[src, C:2 * C]
            acc2[3, dst] += one[src, 2 * C:]

    def finish(f):
        for k, column in enumerate(COLUMNS2):
            flat_acc2[pl.ds(f * PLANE2 + column, H, stride=W), :] = acc2[f, H * W + k * H:H * W + (k + 1) * H]
        own = x_ref[f].reshape(H * W, C).astype(F32)
        o_ref[f] = (own + acc2[f, :H * W]).astype(BF16).reshape(H, W, C)

    def take_sums(parts, sums, copy):
        @pl.when(has_prev)
        def _():
            copy.wait_recv()
        for f in range(2):
            for dst, src in places(parts):
                acc2[f, dst] += sums[f, src].astype(F32)

    for f in range(T):
        stack_inner(2 + f)
    for c in weights_in[:3]:
        c.wait()
    early_hidden(INNER, None)
    for f in (2, 3):
        second_inner(f)
    send_first_rims_late(False)
    for c in weights_in[3:]:
        c.wait()
    make_sums(INNER2, None, qi_out)
    early_share(INNER, None)
    own_share(INNER2, None)
    start_sums(sum_copies[0])
    send_first_rims_late(True)

    take_rims(0, 2, T)
    for f in range(T):
        stack_outer(2 + f)
    early_hidden(OUTER, t1)
    for f in (2, 3):
        second_outer(f)
    make_sums(OUTER2, t2, qo_out)
    start_sums(sum_copies[1])
    early_share(OUTER, t1)
    own_share(OUTER2, t2)

    @pl.when(has_prev)
    def _():
        raw_copy.wait_recv()
    for f in range(2):
        activate(lambda h: prev_raw[f, h], g1, pad1, f * (H + 4) + 2, H)
    send_rims(1, 0, 2)

    for f in range(2):
        stack_inner(f)
    late_hidden(INNER, None)
    for f in range(2):
        second_inner(f)
    late_share(INNER2, None)

    take_rims(1, 0, 2)
    for f in range(2):
        stack_outer(f)
    late_hidden(OUTER, t1)
    for f in range(2):
        second_outer(f)
    late_share(OUTER2, t2)
    finish(2)
    finish(3)
    take_sums(INNER2, qi_in, sum_copies[0])
    take_sums(OUTER2, qo_in, sum_copies[1])
    finish(0)
    finish(1)

    @pl.when(has_next)
    def _():
        for c in [raw_copy] + sum_copies:
            c.wait_send()
    for k in range(2):
        for d, (dr, dc) in enumerate(DIRS):
            @pl.when(exists(dr, dc) if k == 0 else (exists(dr, dc) & has_prev))
            def _():
                rim_copy(k, d).wait_send()


def block(sizes, frames, gain_first, weight_first, gain_second, weight_second):
    T, H, W, C = frames.shape
    hbm = pl.BlockSpec(memory_space=pl.ANY)
    rims = [shape for n in (T, 2) for shape in ((2, n * 2 * W, C),)]
    cols = [shape for n in (T, 2) for shape in ((2, n * 2 * H, C),)]
    corners = [(4, 16, C)] * 2
    return pl.pallas_call(
        functools.partial(kernel, sizes, T, H, W, C),
        out_shape=pltpu.VMEM(frames.shape, frames.dtype),
        in_specs=[hbm] * 5,
        out_specs=pl.BlockSpec(memory_space=pltpu.VMEM),
        scratch_shapes=[
            pltpu.VMEM((T, H, W, C), BF16),
            pltpu.VMEM((1, C), F32),
            pltpu.VMEM((1, C), F32),
            pltpu.VMEM((9 * C, 3 * C), BF16),
            pltpu.VMEM((9 * C, 3 * C), BF16),
            pltpu.VMEM(((T + 2) * (H + 4) + 8, PITCH, C), F32),
            pltpu.VMEM((T * (H + 2), PITCH, C), F32),
            pltpu.VMEM((T + 2, H + 4, W, 3 * C), BF16),
            pltpu.VMEM((T + 2, 4 * SIDE, 9 * C), BF16),
            pltpu.VMEM((T, H + 2, W, 3 * C), BF16),
            pltpu.VMEM((T, 4 * H, 9 * C), BF16),
            pltpu.VMEM((T, (H + 2) * W + 4 * SIDE, C), F32),
            pltpu.VMEM((T, H * W + 4 * H, C), F32),
            pltpu.VMEM((2, H, W, C), BF16),
            pltpu.VMEM((2, (H - 4) * W, C), BF16),
            pltpu.VMEM((2, 4 * W + 4 * H, C), BF16),
            pltpu.VMEM((2, (H - 4) * W, C), BF16),
            pltpu.VMEM((2, 4 * W + 4 * H, C), BF16),
            pltpu.VMEM((4, 16, C), F32),
        ]
        + [pltpu.VMEM(shape, BF16) for shape in (rims + cols + corners) * 2]
        + [
            pltpu.SemaphoreType.DMA((T + 8,)),
            pltpu.SemaphoreType.DMA((3,)),
            pltpu.SemaphoreType.DMA((3,)),
            pltpu.SemaphoreType.DMA((2, len(DIRS))),
            pltpu.SemaphoreType.DMA((2, len(DIRS))),
            pltpu.SemaphoreType.REGULAR((len(DIRS),)),
        ],
        compiler_params=pltpu.CompilerParams(collective_id=0, has_side_effects=True, vmem_limit_bytes=60 * 2**20),
    )(
        frames,
        gain_first.reshape(1, C),
        weight_first.reshape(3, 9 * C, C),
        gain_second.reshape(1, C),
        weight_second.reshape(3, 9 * C, C),
    )


def solution(mesh):
    sizes = dict(mesh.shape)
    return jax.shard_map(
        functools.partial(block, sizes),
        mesh=mesh,
        in_specs=(P("tm", "row", "col", None), P(), P(), P(), P()),
        out_specs=P("tm", "row", "col", None),
        check_vma=False,
    )
```

```python
import functools

import jax
import jax.numpy as jnp
from jax import lax
from jax.experimental import pallas as pl
from jax.experimental.pallas import tpu as pltpu
from jax.sharding import PartitionSpec as P

MESH = pl.DeviceIdType.MESH
F32, BF16 = jnp.float32, jnp.bfloat16
DIRS = ((-1, 0), (1, 0), (0, -1), (0, 1), (-1, -1), (1, -1), (-1, 1), (1, 1))
LEFT = 8
PITCH = 48
SIDE = 24
BARRIER_AT = 0


def act(v, gain):
    half = v * lax.rsqrt(jnp.mean(v * v, axis=-1, keepdims=True) + 1e-6) * (0.5 * gain)
    return half + half * jnp.tanh(half)


def kernel(sizes, T, H, W, C, x_hbm, g1_hbm, w1_hbm, g2_hbm, w2_hbm, o_ref,
           x_ref, g1_ref, g2_ref, w1, w2, pad1, pad2, s1, t1, s2, t2, acc1, acc2, prev_raw, prev_cols, qi_out, qo_out, qi_in, qo_in, stage,
           sr0, sc0, sk0, rr0, rc0, rk0, rr1, rc1,
           local_sem, y_send, y_recv, send_sem, recv_sem, here_sem):
    at = {a: lax.axis_index(a) for a in ("tm", "row", "col")}
    sends, recvs = (sr0, sc0, sk0), (rr0, rc0, rk0)
    flat1 = pad1.reshape(pad1.shape[0] * PITCH, C)
    flat2 = pad2.reshape(pad2.shape[0] * PITCH, C)
    PLANE2 = acc2.shape[1]
    flat_acc2 = acc2.reshape(T * PLANE2, C)
    MAIN = (H + 2) * W
    COLUMNS = (-1, 0, W - 1, W)
    INNER = ((2, H - 2),)
    OUTER = ((0, 2), (H, 2))
    COLUMNS2 = (0, 1, W - 2, W - 1)
    INNER2 = ((2, H - 4),)
    OUTER2 = ((0, 2), (H - 2, 2))

    def exists(dr, dc):
        r, c = at["row"] + dr, at["col"] + dc
        return (r >= 0) & (r < sizes["row"]) & (c >= 0) & (c < sizes["col"])

    def place(dr, dc):
        return {"row": at["row"] + dr, "col": at["col"] + dc}

    has_next, has_prev = at["tm"] + 1 < sizes["tm"], at["tm"] > 0

    frames_in = [pltpu.make_async_copy(x_hbm.at[f], x_ref.at[f], local_sem.at[f]) for f in range(T)]
    gains_in = [pltpu.make_async_copy(g1_hbm, g1_ref, local_sem.at[T]), pltpu.make_async_copy(g2_hbm, g2_ref, local_sem.at[T + 1])]
    weights_in = [
        pltpu.make_async_copy(src.at[kt], dst.at[:, (2 - kt) * C:(3 - kt) * C], local_sem.at[T + 2 + 3 * k + kt])
        for k, (src, dst) in enumerate(((w1_hbm, w1), (w2_hbm, w2))) for kt in range(3)
    ]
    for c in gains_in + frames_in + weights_in:
        c.start()

    for ref in recvs + (rr1, rc1, prev_raw, prev_cols, qi_in, qo_in):
        ref[...] = jnp.zeros_like(ref)

    def is_root(dr, dc):
        return (at["tm"] == 0) & (at["row"] + dr == 0) & (at["col"] + dc == 0)

    def earlier(dr, dc):
        by_place = dc > 0 or (dc == 0 and dr > 0)
        return jnp.logical_not(is_root(0, 0)) if by_place else is_root(dr, dc)

    def later(dr, dc):
        return jnp.logical_not(earlier(dr, dc))

    barrier = pltpu.get_barrier_semaphore()
    expected = has_next.astype(jnp.int32)

    @pl.when(has_prev)
    def _():
        pl.semaphore_signal(barrier, inc=1, device_id={"tm": at["tm"] - 1}, device_id_type=MESH)

    for dr, dc in DIRS:
        @pl.when(exists(dr, dc) & earlier(dr, dc))
        def _():
            pl.semaphore_signal(barrier, inc=1, device_id=place(dr, dc), device_id_type=MESH)
        expected = expected + (exists(dr, dc) & later(dr, dc)).astype(jnp.int32)
    def y_copy(src, dst, k):
        return pltpu.make_async_remote_copy(
            src_ref=src, dst_ref=dst, send_sem=y_send.at[k], recv_sem=y_recv.at[k],
            device_id={"tm": at["tm"] + 1}, device_id_type=MESH)

    edge_copies = [y_copy(x_hbm.at[T - 2:T, h:h + 2], prev_raw.at[:, h:h + 2], 3 + k) for k, h in enumerate((0, H - 2))]
    edge_copies.append(y_copy(sc0.at[:, (T - 2) * 2 * H:], prev_cols, 5))
    raw_copy = y_copy(x_hbm.at[T - 2:T, 2:H - 2], prev_raw.at[:, 2:H - 2], 0)
    sum_copies = [y_copy(qi_out, qi_in, 1), y_copy(qo_out, qo_in, 2)]

    def rim_copy(k, d):
        kind, index = ((0, d), (1, d - 2), (2, d - 4))[(d >= 2) + (d >= 4)]
        if k == 0:
            src, dst = sends[kind].at[index], recvs[kind].at[index]
        elif d < 2:
            src, dst = prev_raw.at[:, (0, H - 2)[d]:(2, H)[d]], rr1.at[d]
        else:
            src, dst = prev_cols.at[int(DIRS[d][1] > 0)], rc1.at[d - 2]
        return pltpu.make_async_remote_copy(
            src_ref=src, dst_ref=dst,
            send_sem=send_sem.at[k, d], recv_sem=recv_sem.at[k, d],
            device_id=place(*DIRS[d]), device_id_type=MESH)

    def send_rims(plane, count):
        rows, cols, corners = sends
        for f in range(count):
            base = (plane + f) * (H + 4) + 2
            for rr in range(2):
                for side, first in ((0, 0), (1, H - 2)):
                    rows[side, (2 * f + rr) * W:(2 * f + rr + 1) * W] = pad1[base + first + rr, LEFT:LEFT + W].astype(BF16)
                for d, top, column in ((0, 0, LEFT), (1, H - 2, LEFT), (2, 0, LEFT + W - 2), (3, H - 2, LEFT + W - 2)):
                    stage[d, 4 * f + 2 * rr:4 * f + 2 * rr + 2] = pad1[base + top + rr, column:column + 2]
            for cc in range(2):
                for side, first in ((0, LEFT), (1, LEFT + W - 2)):
                    cols[side, (2 * f + cc) * H:(2 * f + cc + 1) * H] = flat1[pl.ds(base * PITCH + first + cc, H, stride=PITCH), :].astype(BF16)
        corners[...] = stage[...].astype(BF16)
        for d, (dr, dc) in enumerate(DIRS):
            @pl.when(exists(dr, dc) & later(dr, dc))
            def _():
                rim_copy(0, d).start()

    def hand_on(when):
        @pl.when(has_prev & when)
        def _():
            for c in edge_copies:
                c.wait_recv()
        for d, (dr, dc) in enumerate(DIRS):
            @pl.when(exists(dr, dc) & has_prev & when)
            def _():
                rim_copy(1, d).start()

    def send_first_rims_late(root):
        for d, (dr, dc) in enumerate(DIRS):
            there = is_root(dr, dc)
            @pl.when(exists(dr, dc) & earlier(dr, dc) & (there if root else jnp.logical_not(there)))
            def _():
                pl.semaphore_wait(here_sem.at[d], 1)
                rim_copy(0, d).start()

    def await_rims(k):
        for d, (dr, dc) in enumerate(DIRS):
            @pl.when(exists(-dr, -dc) if k == 0 else (exists(-dr, -dc) & has_prev))
            def _():
                rim_copy(k, d).wait_recv()

    def take_handed_on():
        await_rims(1)
        cols = [rc1[d].astype(F32) for d in range(6)]
        for f in range(2):
            base = f * (H + 4)
            for rr in range(2):
                pad1[base + rr, LEFT:LEFT + W] = act(rr1[1, f, rr].astype(F32), g1)
                pad1[base + H + 2 + rr, LEFT:LEFT + W] = act(rr1[0, f, rr].astype(F32), g1)
            for cc in range(2):
                first = (2 * f + cc) * H
                for d, column in ((1, LEFT - 2), (0, LEFT + W)):
                    flat1[pl.ds((base + 2) * PITCH + column + cc, H, stride=PITCH), :] = cols[d][first:first + H]
                for d, row, top, column in ((5, H - 2, 0, LEFT - 2), (3, H - 2, 0, LEFT + W), (4, 0, H + 2, LEFT - 2), (2, 0, H + 2, LEFT + W)):
                    for rr in range(2):
                        pad1[base + top + rr, column + cc:column + cc + 1] = cols[d][first + row + rr:first + row + rr + 1]

    def take_rims(plane, count):
        await_rims(0)
        rows, cols, corners = recvs
        met = [corners[d].astype(F32) for d in range(4)]
        for f in range(count):
            base = (plane + f) * (H + 4)
            for rr in range(2):
                pad1[base + rr, LEFT:LEFT + W] = rows[1, (2 * f + rr) * W:(2 * f + rr + 1) * W].astype(F32)
                pad1[base + H + 2 + rr, LEFT:LEFT + W] = rows[0, (2 * f + rr) * W:(2 * f + rr + 1) * W].astype(F32)
                for d, top, column in ((3, 0, LEFT - 2), (1, 0, LEFT + W), (2, H + 2, LEFT - 2), (0, H + 2, LEFT + W)):
                    pad1[base + top + rr, column:column + 2] = met[d][4 * f + 2 * rr:4 * f + 2 * rr + 2]
            for cc in range(2):
                for side, first in ((1, LEFT - 2), (0, LEFT + W)):
                    flat1[pl.ds((base + 2) * PITCH + first + cc, H, stride=PITCH), :] = cols[side, (2 * f + cc) * H:(2 * f + cc + 1) * H].astype(F32)

    def activate(load, gain, pad, row0, count):
        for h in range(count):
            pad[row0 + h, LEFT:LEFT + W] = act(load(h).astype(F32), gain)

    def stack(pad, s, plane, row0, h0, count):
        def step(i, _):
            for j in range(2):
                h = h0 + i * 2 + j
                for k in range(3):
                    s[plane, h, :, k * C:(k + 1) * C] = pad[row0 + h, LEFT - 1 + k:LEFT - 1 + k + W].astype(BF16)
            return 0
        lax.fori_loop(0, count // 2, step, 0, unroll=True)

    def stack_inner(plane):
        stack(pad1, s1, plane, plane * (H + 4), 2, H)

    def stack_outer(plane):
        for h0 in (0, H + 2):
            stack(pad1, s1, plane, plane * (H + 4), h0, 2)
        for kh in range(3):
            for kw in range(3):
                rim = [flat1[pl.ds((plane * (H + 4) + kh) * PITCH + LEFT - 1 + column + kw, SIDE, stride=PITCH), :] for column in COLUMNS]
                t1[plane, :, (3 * kh + kw) * C:(3 * kh + kw + 1) * C] = jnp.concatenate(rim, axis=0).astype(BF16)

    def taps(s, plane, w, first, last, parts, side=None):
        lhs = [jnp.concatenate([s[plane, h0 + k:h0 + k + rows].reshape(rows * W, 3 * C) for k in range(3)], axis=1) for h0, rows in parts]
        if side is not None:
            lhs.append(side[plane])
        return jnp.dot(jnp.concatenate(lhs, axis=0), w[:, first * C:(last + 1) * C], preferred_element_type=F32)

    def places(parts):
        n = 0
        for h0, rows in parts:
            yield slice(h0 * W, (h0 + rows) * W), slice(n, n + rows * W)
            n += rows * W
        if parts is OUTER:
            yield slice(MAIN, MAIN + len(COLUMNS) * SIDE), slice(n, n + len(COLUMNS) * SIDE)
        if parts is OUTER2:
            yield slice(H * W, H * W + len(COLUMNS2) * H), slice(n, n + len(COLUMNS2) * H)

    def store_hidden(f, total, parts, final, add=False):
        for dst, src in places(parts):
            value = total[src]
            if add:
                value = value + acc1[f, dst]
            acc1[f, dst] = value.astype(BF16).astype(F32) if final else value

    def second_inner(f):
        activate(lambda h: acc1[f, (2 + h) * W:(3 + h) * W], g2, pad2, f * (H + 2) + 2, H - 2)
        stack(pad2, s2, f, f * (H + 2), 2, H - 2)

    def second_outer(f):
        base = f * (H + 2)
        for h0, rows in OUTER:
            for h in range(h0, h0 + rows):
                pad2[base + h, LEFT:LEFT + W] = act(acc1[f, h * W:(h + 1) * W], g2)
        rim = act(acc1[f, MAIN:], g2)
        for k, column in enumerate(COLUMNS):
            flat2[pl.ds(base * PITCH + LEFT + column, H + 2, stride=PITCH), :] = rim[k * SIDE:k * SIDE + H + 2]
        for column, dc in ((-1, -1), (W, 1)):
            @pl.when(jnp.logical_not(exists(0, dc)))
            def _():
                flat2[pl.ds(base * PITCH + LEFT + column, H + 2, stride=PITCH), :] = jnp.zeros((H + 2, C), F32)
        for h, dr in ((0, -1), (H + 1, 1)):
            @pl.when(jnp.logical_not(exists(dr, 0)))
            def _():
                pad2[base + h] = jnp.zeros((PITCH, C), F32)
        for h0 in (0, H - 2):
            stack(pad2, s2, f, base, h0, 4)
        for kh in range(3):
            for kw in range(3):
                rim = [flat2[pl.ds((base + kh) * PITCH + LEFT - 1 + column + kw, H, stride=PITCH), :] for column in COLUMNS2]
                t2[f, :, (3 * kh + kw) * C:(3 * kh + kw + 1) * C] = jnp.concatenate(rim, axis=0).astype(BF16)

    def early_hidden(parts, side):
        mid = taps(s1, 3, w1, 1, 2, parts, side) + taps(s1, 4, w1, 0, 1, parts, side)
        store_hidden(2, mid[:, :C] + taps(s1, 2, w1, 2, 2, parts, side), parts, True)
        store_hidden(3, mid[:, C:] + taps(s1, 5, w1, 0, 0, parts, side), parts, True)

    def early_share(parts, side):
        part = taps(s1, 2, w1, 0, 1, parts, side)
        store_hidden(0, part[:, :C], parts, False)
        store_hidden(1, part[:, C:] + taps(s1, 3, w1, 0, 0, parts, side), parts, False)

    def late_hidden(parts, side):
        part = taps(s1, 1, w1, 1, 2, parts, side)
        store_hidden(0, part[:, :C] + taps(s1, 0, w1, 2, 2, parts, side), parts, True, True)
        store_hidden(1, part[:, C:], parts, True, True)

    for c in gains_in:
        c.wait()
    g1, g2 = g1_ref[...], g2_ref[...]
    for f in range(T):
        frames_in[f].wait()
        activate(lambda h: x_ref[f, h], g1, pad1, (2 + f) * (H + 4) + 2, H)
        if f == BARRIER_AT:
            @pl.when(expected > 0)
            def _():
                pl.semaphore_wait(barrier, expected)

            @pl.when(has_next)
            def _():
                edge_copies[0].start()
                edge_copies[1].start()

            for d, (dr, dc) in enumerate(DIRS):
                @pl.when(exists(dr, dc) & later(dr, dc))
                def _():
                    pl.semaphore_signal(here_sem.at[DIRS.index((-dr, -dc))], inc=1, device_id=place(dr, dc), device_id_type=MESH)
    send_rims(2, T)

    @pl.when(has_next)
    def _():
        edge_copies[2].start()
        raw_copy.start()

    def make_sums(parts, side, out):
        late = taps(s2, 3, w2, 1, 2, parts, side)
        out[0] = (late[:, :C] + taps(s2, 2, w2, 2, 2, parts, side)).astype(BF16)
        out[1] = late[:, C:].astype(BF16)

    def start_sums(copy):
        @pl.when(has_next)
        def _():
            copy.start()

    def own_share(parts, side):
        part = taps(s2, 2, w2, 0, 1, parts, side)
        other = taps(s2, 3, w2, 0, 0, parts, side)
        for dst, src in places(parts):
            acc2[2, dst] = part[src, :C]
            acc2[3, dst] = part[src, C:] + other[src]

    def late_share(parts, side):
        zero = taps(s2, 0, w2, 0, 2, parts, side)
        one = taps(s2, 1, w2, 0, 2, parts, side)
        for dst, src in places(parts):
            acc2[0, dst] = zero[src, :C]
            acc2[1, dst] = zero[src, C:2 * C] + one[src, :C]
            acc2[2, dst] += zero[src, 2 * C:] + one[src, C:2 * C]
            acc2[3, dst] += one[src, 2 * C:]

    def finish(f):
        for k, column in enumerate(COLUMNS2):
            flat_acc2[pl.ds(f * PLANE2 + column, H, stride=W), :] = acc2[f, H * W + k * H:H * W + (k + 1) * H]
        own = x_ref[f].reshape(H * W, C).astype(F32)
        o_ref[f] = (own + acc2[f, :H * W]).astype(BF16).reshape(H, W, C)

    def take_sums(parts, sums, copy):
        @pl.when(has_prev)
        def _():
            copy.wait_recv()
        for f in range(2):
            for dst, src in places(parts):
                acc2[f, dst] += sums[f, src].astype(F32)

    for f in range(T):
        stack_inner(2 + f)
    for c in weights_in[:3]:
        c.wait()
    early_hidden(INNER, None)
    for f in (2, 3):
        second_inner(f)
    send_first_rims_late(False)
    for c in weights_in[3:]:
        c.wait()
    make_sums(INNER2, None, qi_out)
    early_share(INNER, None)
    start_sums(sum_copies[0])
    send_first_rims_late(True)

    after_root = (at["tm"] == 1) & (at["row"] == 0) & (at["col"] == 0)
    hand_on(jnp.logical_not(after_root))
    take_rims(2, T)
    for f in range(T):
        stack_outer(2 + f)
    early_hidden(OUTER, t1)
    for f in (2, 3):
        second_outer(f)
    make_sums(OUTER2, t2, qo_out)
    start_sums(sum_copies[1])
    hand_on(after_root)
    own_share(INNER2, None)
    early_share(OUTER, t1)
    own_share(OUTER2, t2)

    @pl.when(has_prev)
    def _():
        raw_copy.wait_recv()
    for f in range(2):
        activate(lambda h: prev_raw[f, h], g1, pad1, f * (H + 4) + 2, H)

    for f in range(2):
        stack_inner(f)
    late_hidden(INNER, None)
    for f in range(2):
        second_inner(f)
    late_share(INNER2, None)

    take_handed_on()
    for f in range(2):
        stack_outer(f)
    late_hidden(OUTER, t1)
    for f in range(2):
        second_outer(f)
    late_share(OUTER2, t2)
    finish(2)
    finish(3)
    take_sums(INNER2, qi_in, sum_copies[0])
    take_sums(OUTER2, qo_in, sum_copies[1])
    finish(0)
    finish(1)

    @pl.when(has_next)
    def _():
        for c in [raw_copy] + edge_copies + sum_copies:
            c.wait_send()
    for k in range(2):
        for d, (dr, dc) in enumerate(DIRS):
            @pl.when(exists(dr, dc) if k == 0 else (exists(dr, dc) & has_prev))
            def _():
                rim_copy(k, d).wait_send()


def block(sizes, frames, gain_first, weight_first, gain_second, weight_second):
    T, H, W, C = frames.shape
    hbm = pl.BlockSpec(memory_space=pl.ANY)
    rims = [(2, T * 2 * W, C), (2, T * 2 * H, C), (4, 16, C)]
    return pl.pallas_call(
        functools.partial(kernel, sizes, T, H, W, C),
        out_shape=pltpu.VMEM(frames.shape, frames.dtype),
        in_specs=[hbm] * 5,
        out_specs=pl.BlockSpec(memory_space=pltpu.VMEM),
        scratch_shapes=[
            pltpu.VMEM((T, H, W, C), BF16),
            pltpu.VMEM((1, C), F32),
            pltpu.VMEM((1, C), F32),
            pltpu.VMEM((9 * C, 3 * C), BF16),
            pltpu.VMEM((9 * C, 3 * C), BF16),
            pltpu.VMEM(((T + 2) * (H + 4) + 8, PITCH, C), F32),
            pltpu.VMEM((T * (H + 2), PITCH, C), F32),
            pltpu.VMEM((T + 2, H + 4, W, 3 * C), BF16),
            pltpu.VMEM((T + 2, 4 * SIDE, 9 * C), BF16),
            pltpu.VMEM((T, H + 2, W, 3 * C), BF16),
            pltpu.VMEM((T, 4 * H, 9 * C), BF16),
            pltpu.VMEM((T, (H + 2) * W + 4 * SIDE, C), F32),
            pltpu.VMEM((T, H * W + 4 * H, C), F32),
            pltpu.VMEM((2, H, W, C), BF16),
            pltpu.VMEM((2, 4 * H, C), BF16),
            pltpu.VMEM((2, (H - 4) * W, C), BF16),
            pltpu.VMEM((2, 4 * W + 4 * H, C), BF16),
            pltpu.VMEM((2, (H - 4) * W, C), BF16),
            pltpu.VMEM((2, 4 * W + 4 * H, C), BF16),
            pltpu.VMEM((4, 16, C), F32),
        ]
        + [pltpu.VMEM(shape, BF16) for shape in rims * 2 + [(2, 2, 2, W, C), (6, 4 * H, C)]]
        + [
            pltpu.SemaphoreType.DMA((T + 8,)),
            pltpu.SemaphoreType.DMA((6,)),
            pltpu.SemaphoreType.DMA((6,)),
            pltpu.SemaphoreType.DMA((2, len(DIRS))),
            pltpu.SemaphoreType.DMA((2, len(DIRS))),
            pltpu.SemaphoreType.REGULAR((len(DIRS),)),
        ],
        compiler_params=pltpu.CompilerParams(collective_id=0, has_side_effects=True, vmem_limit_bytes=60 * 2**20),
    )(
        frames,
        gain_first.reshape(1, C),
        weight_first.reshape(3, 9 * C, C),
        gain_second.reshape(1, C),
        weight_second.reshape(3, 9 * C, C),
    )


def solution(mesh):
    sizes = dict(mesh.shape)
    return jax.shard_map(
        functools.partial(block, sizes),
        mesh=mesh,
        in_specs=(P("tm", "row", "col", None), P(), P(), P(), P()),
        out_specs=P("tm", "row", "col", None),
        check_vma=False,
    )
```

```python
import functools

import jax
import jax.numpy as jnp
from jax import lax
from jax.experimental import pallas as pl
from jax.experimental.pallas import tpu as pltpu
from jax.sharding import PartitionSpec as P

MESH = pl.DeviceIdType.MESH
F32, BF16 = jnp.float32, jnp.bfloat16
DIRS = ((-1, 0), (1, 0), (0, -1), (0, 1), (-1, -1), (1, -1), (-1, 1), (1, 1))
LEFT = 8
PITCH = 48
SIDE = 24
BARRIER_AT = 0


def act(v, gain):
    half = v * lax.rsqrt(jnp.mean(v * v, axis=-1, keepdims=True) + 1e-6) * (0.5 * gain)
    return half + half * jnp.tanh(half)


def kernel(sizes, T, H, W, C, x_hbm, g1_hbm, w1_hbm, g2_hbm, w2_hbm, o_ref,
           x_ref, g1_ref, g2_ref, w1, w2, pad1, pad2, s1, t1, s2, t2, acc1, acc2, prev_raw, prev_cols, qi_out, qo_out, qi_in, qo_in, stage, packed,
           sr0, sc0, sk0, rr0, rc0, rk0, rr1, rc1,
           local_sem, y_send, y_recv, send_sem, recv_sem, here_sem):
    at = {a: lax.axis_index(a) for a in ("tm", "row", "col")}
    sends, recvs = (sr0, sc0, sk0), (rr0, rc0, rk0)
    flat1 = pad1.reshape(pad1.shape[0] * PITCH, C)
    flat2 = pad2.reshape(pad2.shape[0] * PITCH, C)
    PLANE2 = acc2.shape[1]
    flat_acc2 = acc2.reshape(T * PLANE2, C)
    MAIN = (H + 2) * W
    COLUMNS = (-1, 0, W - 1, W)
    INNER = ((2, H - 2),)
    OUTER = ((0, 2), (H, 2))
    COLUMNS2 = (0, 1, W - 2, W - 1)
    INNER2 = ((2, H - 4),)
    OUTER2 = ((0, 2), (H - 2, 2))
    MIDDLE = W - 4

    def exists(dr, dc):
        r, c = at["row"] + dr, at["col"] + dc
        return (r >= 0) & (r < sizes["row"]) & (c >= 0) & (c < sizes["col"])

    def place(dr, dc):
        return {"row": at["row"] + dr, "col": at["col"] + dc}

    has_next, has_prev = at["tm"] + 1 < sizes["tm"], at["tm"] > 0

    frames_in = [pltpu.make_async_copy(x_hbm.at[f], x_ref.at[f], local_sem.at[f]) for f in range(T)]
    gains_in = [pltpu.make_async_copy(g1_hbm, g1_ref, local_sem.at[T]), pltpu.make_async_copy(g2_hbm, g2_ref, local_sem.at[T + 1])]
    weights_in = [
        pltpu.make_async_copy(src.at[kt], dst.at[:, (2 - kt) * C:(3 - kt) * C], local_sem.at[T + 2 + 3 * k + kt])
        for k, (src, dst) in enumerate(((w1_hbm, w1), (w2_hbm, w2))) for kt in range(3)
    ]
    for c in gains_in + frames_in + weights_in:
        c.start()

    for ref in recvs + (rr1, rc1, prev_raw, prev_cols, qi_in, qo_in):
        ref[...] = jnp.zeros_like(ref)

    def is_root(dr, dc):
        return (at["tm"] == 0) & (at["row"] + dr == 0) & (at["col"] + dc == 0)

    def earlier(dr, dc):
        by_place = dc > 0 or (dc == 0 and dr > 0)
        return jnp.logical_not(is_root(0, 0)) if by_place else is_root(dr, dc)

    def later(dr, dc):
        return jnp.logical_not(earlier(dr, dc))

    barrier = pltpu.get_barrier_semaphore()
    expected = has_next.astype(jnp.int32)

    @pl.when(has_prev)
    def _():
        pl.semaphore_signal(barrier, inc=1, device_id={"tm": at["tm"] - 1}, device_id_type=MESH)

    for dr, dc in DIRS:
        @pl.when(exists(dr, dc) & earlier(dr, dc))
        def _():
            pl.semaphore_signal(barrier, inc=1, device_id=place(dr, dc), device_id_type=MESH)
        expected = expected + (exists(dr, dc) & later(dr, dc)).astype(jnp.int32)
    def y_copy(src, dst, k):
        return pltpu.make_async_remote_copy(
            src_ref=src, dst_ref=dst, send_sem=y_send.at[k], recv_sem=y_recv.at[k],
            device_id={"tm": at["tm"] + 1}, device_id_type=MESH)

    edge_copies = [y_copy(x_hbm.at[T - 2:T, h:h + 2], prev_raw.at[:, h:h + 2], 3 + k) for k, h in enumerate((0, H - 2))]
    edge_copies.append(y_copy(sc0.at[:, (T - 2) * 2 * H:], prev_cols, 5))
    raw_copy = y_copy(x_hbm.at[T - 2:T, 2:H - 2], prev_raw.at[:, 2:H - 2], 0)
    sum_copies = [y_copy(qi_out, qi_in, 1), y_copy(qo_out, qo_in, 2)]

    def rim_copy(k, d):
        kind, index = ((0, d), (1, d - 2), (2, d - 4))[(d >= 2) + (d >= 4)]
        if k == 0:
            src, dst = sends[kind].at[index], recvs[kind].at[index]
        elif d < 2:
            src, dst = prev_raw.at[:, (0, H - 2)[d]:(2, H)[d]], rr1.at[d]
        else:
            src, dst = prev_cols.at[int(DIRS[d][1] > 0)], rc1.at[d - 2]
        return pltpu.make_async_remote_copy(
            src_ref=src, dst_ref=dst,
            send_sem=send_sem.at[k, d], recv_sem=recv_sem.at[k, d],
            device_id=place(*DIRS[d]), device_id_type=MESH)

    def send_rims(plane, count):
        rows, cols, corners = sends
        for f in range(count):
            base = (plane + f) * (H + 4) + 2
            for rr in range(2):
                for side, first in ((0, 0), (1, H - 2)):
                    rows[side, (2 * f + rr) * W:(2 * f + rr + 1) * W] = pad1[base + first + rr, LEFT:LEFT + W].astype(BF16)
                for d, top, column in ((0, 0, LEFT), (1, H - 2, LEFT), (2, 0, LEFT + W - 2), (3, H - 2, LEFT + W - 2)):
                    stage[d, 4 * f + 2 * rr:4 * f + 2 * rr + 2] = pad1[base + top + rr, column:column + 2]
            for cc in range(2):
                for side, first in ((0, LEFT), (1, LEFT + W - 2)):
                    cols[side, (2 * f + cc) * H:(2 * f + cc + 1) * H] = flat1[pl.ds(base * PITCH + first + cc, H, stride=PITCH), :].astype(BF16)
        corners[...] = stage[...].astype(BF16)
        for d, (dr, dc) in enumerate(DIRS):
            @pl.when(exists(dr, dc) & later(dr, dc))
            def _():
                rim_copy(0, d).start()

    def hand_on(when):
        @pl.when(has_prev & when)
        def _():
            for c in edge_copies:
                c.wait_recv()
        for d, (dr, dc) in enumerate(DIRS):
            @pl.when(exists(dr, dc) & has_prev & when)
            def _():
                rim_copy(1, d).start()

    def send_first_rims_late(root):
        for d, (dr, dc) in enumerate(DIRS):
            there = is_root(dr, dc)
            @pl.when(exists(dr, dc) & earlier(dr, dc) & (there if root else jnp.logical_not(there)))
            def _():
                pl.semaphore_wait(here_sem.at[d], 1)
                rim_copy(0, d).start()

    def await_rims(k):
        for d, (dr, dc) in enumerate(DIRS):
            @pl.when(exists(-dr, -dc) if k == 0 else (exists(-dr, -dc) & has_prev))
            def _():
                rim_copy(k, d).wait_recv()

    def take_handed_on():
        await_rims(1)
        cols = [rc1[d].astype(F32) for d in range(6)]
        for f in range(2):
            base = f * (H + 4)
            for rr in range(2):
                pad1[base + rr, LEFT:LEFT + W] = act(rr1[1, f, rr].astype(F32), g1)
                pad1[base + H + 2 + rr, LEFT:LEFT + W] = act(rr1[0, f, rr].astype(F32), g1)
            for cc in range(2):
                first = (2 * f + cc) * H
                for d, column in ((1, LEFT - 2), (0, LEFT + W)):
                    flat1[pl.ds((base + 2) * PITCH + column + cc, H, stride=PITCH), :] = cols[d][first:first + H]
                for d, row, top, column in ((5, H - 2, 0, LEFT - 2), (3, H - 2, 0, LEFT + W), (4, 0, H + 2, LEFT - 2), (2, 0, H + 2, LEFT + W)):
                    for rr in range(2):
                        pad1[base + top + rr, column + cc:column + cc + 1] = cols[d][first + row + rr:first + row + rr + 1]

    def take_rims(plane, count):
        await_rims(0)
        rows, cols, corners = recvs
        met = [corners[d].astype(F32) for d in range(4)]
        for f in range(count):
            base = (plane + f) * (H + 4)
            for rr in range(2):
                pad1[base + rr, LEFT:LEFT + W] = rows[1, (2 * f + rr) * W:(2 * f + rr + 1) * W].astype(F32)
                pad1[base + H + 2 + rr, LEFT:LEFT + W] = rows[0, (2 * f + rr) * W:(2 * f + rr + 1) * W].astype(F32)
                for d, top, column in ((3, 0, LEFT - 2), (1, 0, LEFT + W), (2, H + 2, LEFT - 2), (0, H + 2, LEFT + W)):
                    pad1[base + top + rr, column:column + 2] = met[d][4 * f + 2 * rr:4 * f + 2 * rr + 2]
            for cc in range(2):
                for side, first in ((1, LEFT - 2), (0, LEFT + W)):
                    flat1[pl.ds((base + 2) * PITCH + first + cc, H, stride=PITCH), :] = cols[side, (2 * f + cc) * H:(2 * f + cc + 1) * H].astype(F32)

    def activate(load, gain, pad, row0, count):
        for h in range(count):
            pad[row0 + h, LEFT:LEFT + W] = act(load(h).astype(F32), gain)

    def stack(pad, s, plane, row0, h0, count):
        def step(i, _):
            for j in range(2):
                h = h0 + i * 2 + j
                for k in range(3):
                    s[plane, h, :, k * C:(k + 1) * C] = pad[row0 + h, LEFT - 1 + k:LEFT - 1 + k + W].astype(BF16)
            return 0
        lax.fori_loop(0, count // 2, step, 0, unroll=True)

    def stack_inner(plane):
        stack(pad1, s1, plane, plane * (H + 4), 2, H)

    def stack_outer(plane):
        for h0 in (0, H + 2):
            stack(pad1, s1, plane, plane * (H + 4), h0, 2)
        for kh in range(3):
            for kw in range(3):
                rim = [flat1[pl.ds((plane * (H + 4) + kh) * PITCH + LEFT - 1 + column + kw, SIDE, stride=PITCH), :] for column in COLUMNS]
                t1[plane, :, (3 * kh + kw) * C:(3 * kh + kw + 1) * C] = jnp.concatenate(rim, axis=0).astype(BF16)

    def taps(s, plane, w, first, last, parts, side=None):
        lhs = [jnp.concatenate([s[plane, h0 + k:h0 + k + rows].reshape(rows * W, 3 * C) for k in range(3)], axis=1) for h0, rows in parts]
        if side is not None:
            lhs.append(side[plane])
        return jnp.dot(jnp.concatenate(lhs, axis=0), w[:, first * C:(last + 1) * C], preferred_element_type=F32)

    def places(parts):
        n = 0
        for h0, rows in parts:
            yield slice(h0 * W, (h0 + rows) * W), slice(n, n + rows * W)
            n += rows * W
        if parts is OUTER:
            yield slice(MAIN, MAIN + len(COLUMNS) * SIDE), slice(n, n + len(COLUMNS) * SIDE)
        if parts is OUTER2:
            yield slice(H * W, H * W + len(COLUMNS2) * H), slice(n, n + len(COLUMNS2) * H)

    def store_hidden(f, total, parts, final, add=False):
        for dst, src in places(parts):
            value = total[src]
            if add:
                value = value + acc1[f, dst]
            acc1[f, dst] = value.astype(BF16).astype(F32) if final else value

    def second_inner(f):
        activate(lambda h: acc1[f, (2 + h) * W:(3 + h) * W], g2, pad2, f * (H + 2) + 2, H - 2)
        stack(pad2, s2, f, f * (H + 2), 2, H - 2)

    def second_outer(f):
        base = f * (H + 2)
        for h0, rows in OUTER:
            for h in range(h0, h0 + rows):
                pad2[base + h, LEFT:LEFT + W] = act(acc1[f, h * W:(h + 1) * W], g2)
        rim = act(acc1[f, MAIN:], g2)
        for k, column in enumerate(COLUMNS):
            flat2[pl.ds(base * PITCH + LEFT + column, H + 2, stride=PITCH), :] = rim[k * SIDE:k * SIDE + H + 2]
        for column, dc in ((-1, -1), (W, 1)):
            @pl.when(jnp.logical_not(exists(0, dc)))
            def _():
                flat2[pl.ds(base * PITCH + LEFT + column, H + 2, stride=PITCH), :] = jnp.zeros((H + 2, C), F32)
        for h, dr in ((0, -1), (H + 1, 1)):
            @pl.when(jnp.logical_not(exists(dr, 0)))
            def _():
                pad2[base + h] = jnp.zeros((PITCH, C), F32)
        for h0 in (0, H - 2):
            stack(pad2, s2, f, base, h0, 4)
        for kh in range(3):
            for kw in range(3):
                rim = [flat2[pl.ds((base + kh) * PITCH + LEFT - 1 + column + kw, H, stride=PITCH), :] for column in COLUMNS2]
                t2[f, :, (3 * kh + kw) * C:(3 * kh + kw + 1) * C] = jnp.concatenate(rim, axis=0).astype(BF16)

    def early_hidden(parts, side):
        mid = taps(s1, 3, w1, 1, 2, parts, side) + taps(s1, 4, w1, 0, 1, parts, side)
        store_hidden(2, mid[:, :C] + taps(s1, 2, w1, 2, 2, parts, side), parts, True)
        store_hidden(3, mid[:, C:] + taps(s1, 5, w1, 0, 0, parts, side), parts, True)

    def early_share(parts, side):
        part = taps(s1, 2, w1, 0, 1, parts, side)
        store_hidden(0, part[:, :C], parts, False)
        store_hidden(1, part[:, C:] + taps(s1, 3, w1, 0, 0, parts, side), parts, False)

    def late_hidden(parts, side):
        part = taps(s1, 1, w1, 1, 2, parts, side)
        store_hidden(0, part[:, :C] + taps(s1, 0, w1, 2, 2, parts, side), parts, True, True)
        store_hidden(1, part[:, C:], parts, True, True)

    for c in gains_in:
        c.wait()
    g1, g2 = g1_ref[...], g2_ref[...]
    for f in range(T):
        frames_in[f].wait()
        if f == BARRIER_AT:
            @pl.when(expected > 0)
            def _():
                pl.semaphore_wait(barrier, expected)

            @pl.when(has_next)
            def _():
                edge_copies[0].start()
                edge_copies[1].start()

            for d, (dr, dc) in enumerate(DIRS):
                @pl.when(exists(dr, dc) & later(dr, dc))
                def _():
                    pl.semaphore_signal(here_sem.at[DIRS.index((-dr, -dc))], inc=1, device_id=place(dr, dc), device_id_type=MESH)
        activate(lambda h: x_ref[f, h], g1, pad1, (2 + f) * (H + 4) + 2, H)
    send_rims(2, T)

    @pl.when(has_next)
    def _():
        edge_copies[2].start()
        raw_copy.start()

    def make_sums(parts, side, out):
        late = taps(s2, 3, w2, 1, 2, parts, side)
        out[0] = (late[:, :C] + taps(s2, 2, w2, 2, 2, parts, side)).astype(BF16)
        out[1] = late[:, C:].astype(BF16)

    def make_inner_sums():
        late = taps(s2, 3, w2, 1, 2, INNER2)
        for f, value in enumerate((late[:, :C] + taps(s2, 2, w2, 2, 2, INNER2), late[:, C:])):
            for i in range(H - 4):
                packed[f, i * MIDDLE:(i + 1) * MIDDLE] = value[i * W + 2:i * W + 2 + MIDDLE]
            qi_out[f] = packed[f].astype(BF16)

    def start_sums(copy):
        @pl.when(has_next)
        def _():
            copy.start()

    def own_share(parts, side):
        part = taps(s2, 2, w2, 0, 1, parts, side)
        other = taps(s2, 3, w2, 0, 0, parts, side)
        for dst, src in places(parts):
            acc2[2, dst] = part[src, :C]
            acc2[3, dst] = part[src, C:] + other[src]

    def late_share(parts, side):
        zero = taps(s2, 0, w2, 0, 2, parts, side)
        one = taps(s2, 1, w2, 0, 2, parts, side)
        for dst, src in places(parts):
            acc2[0, dst] = zero[src, :C]
            acc2[1, dst] = zero[src, C:2 * C] + one[src, :C]
            acc2[2, dst] += zero[src, 2 * C:] + one[src, C:2 * C]
            acc2[3, dst] += one[src, 2 * C:]

    def finish(f):
        for k, column in enumerate(COLUMNS2):
            flat_acc2[pl.ds(f * PLANE2 + column, H, stride=W), :] = acc2[f, H * W + k * H:H * W + (k + 1) * H]
        own = x_ref[f].reshape(H * W, C).astype(F32)
        o_ref[f] = (own + acc2[f, :H * W]).astype(BF16).reshape(H, W, C)

    def take_sums(parts, sums, copy):
        @pl.when(has_prev)
        def _():
            copy.wait_recv()
        for f in range(2):
            for dst, src in places(parts):
                acc2[f, dst] += sums[f, src].astype(F32)

    def take_inner_sums():
        @pl.when(has_prev)
        def _():
            sum_copies[0].wait_recv()
        for f in range(2):
            packed[f] = qi_in[f].astype(F32)
            for i in range(H - 4):
                first = (2 + i) * W + 2
                acc2[f, first:first + MIDDLE] += packed[f, i * MIDDLE:(i + 1) * MIDDLE]

    for f in range(T):
        stack_inner(2 + f)
    for c in weights_in[:3]:
        c.wait()
    early_hidden(INNER, None)
    for f in (2, 3):
        second_inner(f)
    send_first_rims_late(False)
    for c in weights_in[3:]:
        c.wait()
    make_inner_sums()
    start_sums(sum_copies[0])
    early_share(INNER, None)
    own_share(INNER2, None)
    send_first_rims_late(True)

    after_root = (at["tm"] == 1) & (at["row"] == 0) & (at["col"] == 0)
    hand_on(jnp.logical_not(after_root))
    take_rims(2, T)
    for f in range(T):
        stack_outer(2 + f)
    early_hidden(OUTER, t1)
    for f in (2, 3):
        second_outer(f)
    make_sums(OUTER2, t2, qo_out)
    start_sums(sum_copies[1])
    hand_on(after_root)
    early_share(OUTER, t1)
    own_share(OUTER2, t2)

    @pl.when(has_prev)
    def _():
        raw_copy.wait_recv()
    for f in range(2):
        activate(lambda h: prev_raw[f, h], g1, pad1, f * (H + 4) + 2, H)

    for f in range(2):
        stack_inner(f)
    late_hidden(INNER, None)
    for f in range(2):
        second_inner(f)
    late_share(INNER2, None)

    take_handed_on()
    for f in range(2):
        stack_outer(f)
    late_hidden(OUTER, t1)
    for f in range(2):
        second_outer(f)
    late_share(OUTER2, t2)
    finish(2)
    finish(3)
    take_inner_sums()
    take_sums(OUTER2, qo_in, sum_copies[1])
    finish(0)
    finish(1)

    @pl.when(has_next)
    def _():
        for c in [raw_copy] + edge_copies + sum_copies:
            c.wait_send()
    for k in range(2):
        for d, (dr, dc) in enumerate(DIRS):
            @pl.when(exists(dr, dc) if k == 0 else (exists(dr, dc) & has_prev))
            def _():
                rim_copy(k, d).wait_send()


def block(sizes, frames, gain_first, weight_first, gain_second, weight_second):
    T, H, W, C = frames.shape
    hbm = pl.BlockSpec(memory_space=pl.ANY)
    rims = [(2, T * 2 * W, C), (2, T * 2 * H, C), (4, 16, C)]
    return pl.pallas_call(
        functools.partial(kernel, sizes, T, H, W, C),
        out_shape=pltpu.VMEM(frames.shape, frames.dtype),
        in_specs=[hbm] * 5,
        out_specs=pl.BlockSpec(memory_space=pltpu.VMEM),
        scratch_shapes=[
            pltpu.VMEM((T, H, W, C), BF16),
            pltpu.VMEM((1, C), F32),
            pltpu.VMEM((1, C), F32),
            pltpu.VMEM((9 * C, 3 * C), BF16),
            pltpu.VMEM((9 * C, 3 * C), BF16),
            pltpu.VMEM(((T + 2) * (H + 4) + 8, PITCH, C), F32),
            pltpu.VMEM((T * (H + 2) + 1, PITCH, C), F32),
            pltpu.VMEM((T + 2, H + 4, W, 3 * C), BF16),
            pltpu.VMEM((T + 2, 4 * SIDE, 9 * C), BF16),
            pltpu.VMEM((T, H + 2, W, 3 * C), BF16),
            pltpu.VMEM((T, 4 * H, 9 * C), BF16),
            pltpu.VMEM((T, (H + 2) * W + 4 * SIDE, C), F32),
            pltpu.VMEM((T, H * W + 4 * H, C), F32),
            pltpu.VMEM((2, H, W, C), BF16),
            pltpu.VMEM((2, 4 * H, C), BF16),
            pltpu.VMEM((2, (H - 4) * (W - 4), C), BF16),
            pltpu.VMEM((2, 4 * W + 4 * H, C), BF16),
            pltpu.VMEM((2, (H - 4) * (W - 4), C), BF16),
            pltpu.VMEM((2, 4 * W + 4 * H, C), BF16),
            pltpu.VMEM((4, 16, C), F32),
            pltpu.VMEM((2, (H - 4) * (W - 4), C), F32),
        ]
        + [pltpu.VMEM(shape, BF16) for shape in rims * 2 + [(2, 2, 2, W, C), (6, 4 * H, C)]]
        + [
            pltpu.SemaphoreType.DMA((T + 8,)),
            pltpu.SemaphoreType.DMA((6,)),
            pltpu.SemaphoreType.DMA((6,)),
            pltpu.SemaphoreType.DMA((2, len(DIRS))),
            pltpu.SemaphoreType.DMA((2, len(DIRS))),
            pltpu.SemaphoreType.REGULAR((len(DIRS),)),
        ],
        compiler_params=pltpu.CompilerParams(collective_id=0, has_side_effects=True, vmem_limit_bytes=60 * 2**20),
    )(
        frames,
        gain_first.reshape(1, C),
        weight_first.reshape(3, 9 * C, C),
        gain_second.reshape(1, C),
        weight_second.reshape(3, 9 * C, C),
    )


def solution(mesh):
    sizes = dict(mesh.shape)
    return jax.shard_map(
        functools.partial(block, sizes),
        mesh=mesh,
        in_specs=(P("tm", "row", "col", None), P(), P(), P(), P()),
        out_specs=P("tm", "row", "col", None),
        check_vma=False,
    )
```

```python
import functools

import jax
import jax.numpy as jnp
from jax import lax
from jax.experimental import pallas as pl
from jax.experimental.pallas import tpu as pltpu
from jax.sharding import PartitionSpec as P

MESH = pl.DeviceIdType.MESH
F32, BF16 = jnp.float32, jnp.bfloat16
DIRS = ((-1, 0), (1, 0), (0, -1), (0, 1), (-1, -1), (1, -1), (-1, 1), (1, 1))
LEFT = 8
PITCH = 48
SIDE = 24
BARRIER_AT = 0


def act(v, gain):
    half = v * lax.rsqrt(jnp.mean(v * v, axis=-1, keepdims=True) + 1e-6) * (0.5 * gain)
    return half + half * jnp.tanh(half)


def kernel(sizes, T, H, W, C, x_hbm, g1_hbm, w1_hbm, g2_hbm, w2_hbm, o_ref,
           x_ref, g1_ref, g2_ref, w1, w2, pad1, pad2, s1, t1, s2, t2, acc1, acc2, prev_raw, prev_cols, qi_out, qo_out, qi_in, qo_in, stage, packed,
           sr0, sc0, sk0, rr0, rc0, rk0, rr1, rc1,
           local_sem, y_send, y_recv, send_sem, recv_sem, here_sem):
    at = {a: lax.axis_index(a) for a in ("tm", "row", "col")}
    sends, recvs = (sr0, sc0, sk0), (rr0, rc0, rk0)
    flat1 = pad1.reshape(pad1.shape[0] * PITCH, C)
    flat2 = pad2.reshape(pad2.shape[0] * PITCH, C)
    PLANE2 = acc2.shape[1]
    flat_acc2 = acc2.reshape(T * PLANE2, C)
    MAIN = (H + 2) * W
    COLUMNS = (-1, 0, W - 1, W)
    INNER = ((2, H - 2),)
    OUTER = ((0, 2), (H, 2))
    COLUMNS2 = (0, 1, W - 2, W - 1)
    INNER2 = ((2, H - 4),)
    OUTER2 = ((0, 2), (H - 2, 2))
    MIDDLE = W - 4

    def exists(dr, dc):
        r, c = at["row"] + dr, at["col"] + dc
        return (r >= 0) & (r < sizes["row"]) & (c >= 0) & (c < sizes["col"])

    def place(dr, dc):
        return {"row": at["row"] + dr, "col": at["col"] + dc}

    has_next, has_prev = at["tm"] + 1 < sizes["tm"], at["tm"] > 0

    frames_in = [pltpu.make_async_copy(x_hbm.at[f], x_ref.at[f], local_sem.at[f]) for f in range(T)]
    gains_in = [pltpu.make_async_copy(g1_hbm, g1_ref, local_sem.at[T]), pltpu.make_async_copy(g2_hbm, g2_ref, local_sem.at[T + 1])]
    weights_in = [
        pltpu.make_async_copy(src.at[kt], dst.at[:, (2 - kt) * C:(3 - kt) * C], local_sem.at[T + 2 + 3 * k + kt])
        for k, (src, dst) in enumerate(((w1_hbm, w1), (w2_hbm, w2))) for kt in range(3)
    ]
    for c in gains_in + frames_in:
        c.start()

    for ref in recvs + (rr1, rc1, prev_raw, prev_cols, qi_in, qo_in):
        ref[...] = jnp.zeros_like(ref)

    def is_root(dr, dc):
        return (at["tm"] == 0) & (at["row"] + dr == 0) & (at["col"] + dc == 0)

    def earlier(dr, dc):
        by_place = dc > 0 or (dc == 0 and dr > 0)
        return jnp.logical_not(is_root(0, 0)) if by_place else is_root(dr, dc)

    def later(dr, dc):
        return jnp.logical_not(earlier(dr, dc))

    barrier = pltpu.get_barrier_semaphore()
    expected = has_next.astype(jnp.int32)

    @pl.when(has_prev)
    def _():
        pl.semaphore_signal(barrier, inc=1, device_id={"tm": at["tm"] - 1}, device_id_type=MESH)

    for dr, dc in DIRS:
        @pl.when(exists(dr, dc) & earlier(dr, dc))
        def _():
            pl.semaphore_signal(barrier, inc=1, device_id=place(dr, dc), device_id_type=MESH)
        expected = expected + (exists(dr, dc) & later(dr, dc)).astype(jnp.int32)
    def y_copy(src, dst, k):
        return pltpu.make_async_remote_copy(
            src_ref=src, dst_ref=dst, send_sem=y_send.at[k], recv_sem=y_recv.at[k],
            device_id={"tm": at["tm"] + 1}, device_id_type=MESH)

    edge_copies = [y_copy(x_hbm.at[T - 2:T, h:h + 2], prev_raw.at[:, h:h + 2], 3 + k) for k, h in enumerate((0, H - 2))]
    edge_copies.append(y_copy(sc0.at[:, (T - 2) * 2 * H:], prev_cols, 5))
    raw_copy = y_copy(x_hbm.at[T - 2:T, 2:H - 2], prev_raw.at[:, 2:H - 2], 0)
    sum_copies = [y_copy(qi_out, qi_in, 1), y_copy(qo_out, qo_in, 2)]

    def rim_copy(k, d):
        kind, index = ((0, d), (1, d - 2), (2, d - 4))[(d >= 2) + (d >= 4)]
        if k == 0:
            src, dst = sends[kind].at[index], recvs[kind].at[index]
        elif d < 2:
            src, dst = prev_raw.at[:, (0, H - 2)[d]:(2, H)[d]], rr1.at[d]
        else:
            src, dst = prev_cols.at[int(DIRS[d][1] > 0)], rc1.at[d - 2]
        return pltpu.make_async_remote_copy(
            src_ref=src, dst_ref=dst,
            send_sem=send_sem.at[k, d], recv_sem=recv_sem.at[k, d],
            device_id=place(*DIRS[d]), device_id_type=MESH)

    def send_rims(plane, count):
        rows, cols, corners = sends
        for f in range(count):
            base = (plane + f) * (H + 4) + 2
            for rr in range(2):
                for side, first in ((0, 0), (1, H - 2)):
                    rows[side, (2 * f + rr) * W:(2 * f + rr + 1) * W] = pad1[base + first + rr, LEFT:LEFT + W].astype(BF16)
                for d, top, column in ((0, 0, LEFT), (1, H - 2, LEFT), (2, 0, LEFT + W - 2), (3, H - 2, LEFT + W - 2)):
                    stage[d, 4 * f + 2 * rr:4 * f + 2 * rr + 2] = pad1[base + top + rr, column:column + 2]
            for cc in range(2):
                for side, first in ((0, LEFT), (1, LEFT + W - 2)):
                    cols[side, (2 * f + cc) * H:(2 * f + cc + 1) * H] = flat1[pl.ds(base * PITCH + first + cc, H, stride=PITCH), :].astype(BF16)
        corners[...] = stage[...].astype(BF16)
        for d, (dr, dc) in enumerate(DIRS):
            @pl.when(exists(dr, dc) & later(dr, dc))
            def _():
                rim_copy(0, d).start()

    def hand_on(when):
        @pl.when(has_prev & when)
        def _():
            for c in edge_copies:
                c.wait_recv()
        for d, (dr, dc) in enumerate(DIRS):
            @pl.when(exists(dr, dc) & has_prev & when)
            def _():
                rim_copy(1, d).start()

    def send_first_rims_late(root):
        for d, (dr, dc) in enumerate(DIRS):
            there = is_root(dr, dc)
            @pl.when(exists(dr, dc) & earlier(dr, dc) & (there if root else jnp.logical_not(there)))
            def _():
                pl.semaphore_wait(here_sem.at[d], 1)
                rim_copy(0, d).start()

    def await_rims(k):
        for d, (dr, dc) in enumerate(DIRS):
            @pl.when(exists(-dr, -dc) if k == 0 else (exists(-dr, -dc) & has_prev))
            def _():
                rim_copy(k, d).wait_recv()

    def take_handed_on():
        await_rims(1)
        cols = [rc1[d].astype(F32) for d in range(6)]
        for f in range(2):
            base = f * (H + 4)
            for rr in range(2):
                pad1[base + rr, LEFT:LEFT + W] = act(rr1[1, f, rr].astype(F32), g1)
                pad1[base + H + 2 + rr, LEFT:LEFT + W] = act(rr1[0, f, rr].astype(F32), g1)
            for cc in range(2):
                first = (2 * f + cc) * H
                for d, column in ((1, LEFT - 2), (0, LEFT + W)):
                    flat1[pl.ds((base + 2) * PITCH + column + cc, H, stride=PITCH), :] = cols[d][first:first + H]
                for d, row, top, column in ((5, H - 2, 0, LEFT - 2), (3, H - 2, 0, LEFT + W), (4, 0, H + 2, LEFT - 2), (2, 0, H + 2, LEFT + W)):
                    for rr in range(2):
                        pad1[base + top + rr, column + cc:column + cc + 1] = cols[d][first + row + rr:first + row + rr + 1]

    def take_rims(plane, count):
        await_rims(0)
        rows, cols, corners = recvs
        met = [corners[d].astype(F32) for d in range(4)]
        for f in range(count):
            base = (plane + f) * (H + 4)
            for rr in range(2):
                pad1[base + rr, LEFT:LEFT + W] = rows[1, (2 * f + rr) * W:(2 * f + rr + 1) * W].astype(F32)
                pad1[base + H + 2 + rr, LEFT:LEFT + W] = rows[0, (2 * f + rr) * W:(2 * f + rr + 1) * W].astype(F32)
                for d, top, column in ((3, 0, LEFT - 2), (1, 0, LEFT + W), (2, H + 2, LEFT - 2), (0, H + 2, LEFT + W)):
                    pad1[base + top + rr, column:column + 2] = met[d][4 * f + 2 * rr:4 * f + 2 * rr + 2]
            for cc in range(2):
                for side, first in ((1, LEFT - 2), (0, LEFT + W)):
                    flat1[pl.ds((base + 2) * PITCH + first + cc, H, stride=PITCH), :] = cols[side, (2 * f + cc) * H:(2 * f + cc + 1) * H].astype(F32)

    def activate(load, gain, pad, row0, count):
        for h in range(count):
            pad[row0 + h, LEFT:LEFT + W] = act(load(h).astype(F32), gain)

    def stack(pad, s, plane, row0, h0, count):
        def step(i, _):
            for j in range(2):
                h = h0 + i * 2 + j
                for k in range(3):
                    s[plane, h, :, k * C:(k + 1) * C] = pad[row0 + h, LEFT - 1 + k:LEFT - 1 + k + W].astype(BF16)
            return 0
        lax.fori_loop(0, count // 2, step, 0, unroll=True)

    def stack_inner(plane):
        stack(pad1, s1, plane, plane * (H + 4), 2, H)

    def stack_outer(plane):
        for h0 in (0, H + 2):
            stack(pad1, s1, plane, plane * (H + 4), h0, 2)
        for kh in range(3):
            for kw in range(3):
                rim = [flat1[pl.ds((plane * (H + 4) + kh) * PITCH + LEFT - 1 + column + kw, SIDE, stride=PITCH), :] for column in COLUMNS]
                t1[plane, :, (3 * kh + kw) * C:(3 * kh + kw + 1) * C] = jnp.concatenate(rim, axis=0).astype(BF16)

    def taps(s, plane, w, first, last, parts, side=None):
        lhs = [jnp.concatenate([s[plane, h0 + k:h0 + k + rows].reshape(rows * W, 3 * C) for k in range(3)], axis=1) for h0, rows in parts]
        if side is not None:
            lhs.append(side[plane])
        return jnp.dot(jnp.concatenate(lhs, axis=0), w[:, first * C:(last + 1) * C], preferred_element_type=F32)

    def places(parts):
        n = 0
        for h0, rows in parts:
            yield slice(h0 * W, (h0 + rows) * W), slice(n, n + rows * W)
            n += rows * W
        if parts is OUTER:
            yield slice(MAIN, MAIN + len(COLUMNS) * SIDE), slice(n, n + len(COLUMNS) * SIDE)
        if parts is OUTER2:
            yield slice(H * W, H * W + len(COLUMNS2) * H), slice(n, n + len(COLUMNS2) * H)

    def store_hidden(f, total, parts, final, add=False):
        for dst, src in places(parts):
            value = total[src]
            if add:
                value = value + acc1[f, dst]
            acc1[f, dst] = value.astype(BF16).astype(F32) if final else value

    def second_inner(f):
        activate(lambda h: acc1[f, (2 + h) * W:(3 + h) * W], g2, pad2, f * (H + 2) + 2, H - 2)
        stack(pad2, s2, f, f * (H + 2), 2, H - 2)

    def second_outer(f):
        base = f * (H + 2)
        for h0, rows in OUTER:
            for h in range(h0, h0 + rows):
                pad2[base + h, LEFT:LEFT + W] = act(acc1[f, h * W:(h + 1) * W], g2)
        rim = act(acc1[f, MAIN:], g2)
        for k, column in enumerate(COLUMNS):
            flat2[pl.ds(base * PITCH + LEFT + column, H + 2, stride=PITCH), :] = rim[k * SIDE:k * SIDE + H + 2]
        for column, dc in ((-1, -1), (W, 1)):
            @pl.when(jnp.logical_not(exists(0, dc)))
            def _():
                flat2[pl.ds(base * PITCH + LEFT + column, H + 2, stride=PITCH), :] = jnp.zeros((H + 2, C), F32)
        for h, dr in ((0, -1), (H + 1, 1)):
            @pl.when(jnp.logical_not(exists(dr, 0)))
            def _():
                pad2[base + h] = jnp.zeros((PITCH, C), F32)
        for h0 in (0, H - 2):
            stack(pad2, s2, f, base, h0, 4)
        for kh in range(3):
            for kw in range(3):
                rim = [flat2[pl.ds((base + kh) * PITCH + LEFT - 1 + column + kw, H, stride=PITCH), :] for column in COLUMNS2]
                t2[f, :, (3 * kh + kw) * C:(3 * kh + kw + 1) * C] = jnp.concatenate(rim, axis=0).astype(BF16)

    def early_hidden(parts, side):
        mid = taps(s1, 3, w1, 1, 2, parts, side) + taps(s1, 4, w1, 0, 1, parts, side)
        store_hidden(2, mid[:, :C] + taps(s1, 2, w1, 2, 2, parts, side), parts, True)
        store_hidden(3, mid[:, C:] + taps(s1, 5, w1, 0, 0, parts, side), parts, True)

    def early_share(parts, side):
        part = taps(s1, 2, w1, 0, 1, parts, side)
        store_hidden(0, part[:, :C], parts, False)
        store_hidden(1, part[:, C:] + taps(s1, 3, w1, 0, 0, parts, side), parts, False)

    def late_hidden(parts, side):
        part = taps(s1, 1, w1, 1, 2, parts, side)
        store_hidden(0, part[:, :C] + taps(s1, 0, w1, 2, 2, parts, side), parts, True, True)
        store_hidden(1, part[:, C:], parts, True, True)

    for c in gains_in:
        c.wait()
    g1, g2 = g1_ref[...], g2_ref[...]
    for f in range(T):
        frames_in[f].wait()
        if f == BARRIER_AT:
            @pl.when(expected > 0)
            def _():
                pl.semaphore_wait(barrier, expected)

            @pl.when(has_next)
            def _():
                edge_copies[0].start()
                edge_copies[1].start()

            for d, (dr, dc) in enumerate(DIRS):
                @pl.when(exists(dr, dc) & later(dr, dc))
                def _():
                    pl.semaphore_signal(here_sem.at[DIRS.index((-dr, -dc))], inc=1, device_id=place(dr, dc), device_id_type=MESH)
        if f == 1:
            for c in weights_in:
                c.start()
        activate(lambda h: x_ref[f, h], g1, pad1, (2 + f) * (H + 4) + 2, H)
    send_rims(2, T)

    @pl.when(has_next)
    def _():
        edge_copies[2].start()
        raw_copy.start()

    def make_sums(parts, side, out):
        late = taps(s2, 3, w2, 1, 2, parts, side)
        out[0] = (late[:, :C] + taps(s2, 2, w2, 2, 2, parts, side)).astype(BF16)
        out[1] = late[:, C:].astype(BF16)

    def make_inner_sums():
        late = taps(s2, 3, w2, 1, 2, INNER2)
        for f, value in enumerate((late[:, :C] + taps(s2, 2, w2, 2, 2, INNER2), late[:, C:])):
            for i in range(H - 4):
                packed[f, i * MIDDLE:(i + 1) * MIDDLE] = value[i * W + 2:i * W + 2 + MIDDLE]
            qi_out[f] = packed[f].astype(BF16)

    def start_sums(copy):
        @pl.when(has_next)
        def _():
            copy.start()

    def own_share(parts, side):
        part = taps(s2, 2, w2, 0, 1, parts, side)
        other = taps(s2, 3, w2, 0, 0, parts, side)
        for dst, src in places(parts):
            acc2[2, dst] = part[src, :C]
            acc2[3, dst] = part[src, C:] + other[src]

    def late_share(parts, side):
        zero = taps(s2, 0, w2, 0, 2, parts, side)
        one = taps(s2, 1, w2, 0, 2, parts, side)
        for dst, src in places(parts):
            acc2[0, dst] = zero[src, :C]
            acc2[1, dst] = zero[src, C:2 * C] + one[src, :C]
            acc2[2, dst] += zero[src, 2 * C:] + one[src, C:2 * C]
            acc2[3, dst] += one[src, 2 * C:]

    def finish(f):
        for k, column in enumerate(COLUMNS2):
            flat_acc2[pl.ds(f * PLANE2 + column, H, stride=W), :] = acc2[f, H * W + k * H:H * W + (k + 1) * H]
        own = x_ref[f].reshape(H * W, C).astype(F32)
        o_ref[f] = (own + acc2[f, :H * W]).astype(BF16).reshape(H, W, C)

    def take_sums(parts, sums, copy):
        @pl.when(has_prev)
        def _():
            copy.wait_recv()
        for f in range(2):
            for dst, src in places(parts):
                acc2[f, dst] += sums[f, src].astype(F32)

    def take_inner_sums():
        @pl.when(has_prev)
        def _():
            sum_copies[0].wait_recv()
        for f in range(2):
            packed[f] = qi_in[f].astype(F32)
            for i in range(H - 4):
                first = (2 + i) * W + 2
                acc2[f, first:first + MIDDLE] += packed[f, i * MIDDLE:(i + 1) * MIDDLE]

    for f in range(T):
        stack_inner(2 + f)
    for c in weights_in[:3]:
        c.wait()
    early_hidden(INNER, None)
    for f in (2, 3):
        second_inner(f)
    send_first_rims_late(False)
    for c in weights_in[3:]:
        c.wait()
    make_inner_sums()
    start_sums(sum_copies[0])
    early_share(INNER, None)
    own_share(INNER2, None)
    send_first_rims_late(True)

    after_root = (at["tm"] == 1) & (at["row"] == 0) & (at["col"] == 0)
    hand_on(jnp.logical_not(after_root))
    take_rims(2, T)
    for f in range(T):
        stack_outer(2 + f)
    early_hidden(OUTER, t1)
    for f in (2, 3):
        second_outer(f)
    make_sums(OUTER2, t2, qo_out)
    start_sums(sum_copies[1])
    hand_on(after_root)
    early_share(OUTER, t1)
    own_share(OUTER2, t2)

    @pl.when(has_prev)
    def _():
        raw_copy.wait_recv()
    for f in range(2):
        activate(lambda h: prev_raw[f, h], g1, pad1, f * (H + 4) + 2, H)

    for f in range(2):
        stack_inner(f)
    late_hidden(INNER, None)
    for f in range(2):
        second_inner(f)
    late_share(INNER2, None)

    take_handed_on()
    for f in range(2):
        stack_outer(f)
    late_hidden(OUTER, t1)
    for f in range(2):
        second_outer(f)
    late_share(OUTER2, t2)
    finish(2)
    finish(3)
    take_inner_sums()
    take_sums(OUTER2, qo_in, sum_copies[1])
    finish(0)
    finish(1)

    @pl.when(has_next)
    def _():
        for c in [raw_copy] + edge_copies + sum_copies:
            c.wait_send()
    for k in range(2):
        for d, (dr, dc) in enumerate(DIRS):
            @pl.when(exists(dr, dc) if k == 0 else (exists(dr, dc) & has_prev))
            def _():
                rim_copy(k, d).wait_send()


def block(sizes, frames, gain_first, weight_first, gain_second, weight_second):
    T, H, W, C = frames.shape
    hbm = pl.BlockSpec(memory_space=pl.ANY)
    rims = [(2, T * 2 * W, C), (2, T * 2 * H, C), (4, 16, C)]
    return pl.pallas_call(
        functools.partial(kernel, sizes, T, H, W, C),
        out_shape=pltpu.VMEM(frames.shape, frames.dtype),
        in_specs=[hbm] * 5,
        out_specs=pl.BlockSpec(memory_space=pltpu.VMEM),
        scratch_shapes=[
            pltpu.VMEM((T, H, W, C), BF16),
            pltpu.VMEM((1, C), F32),
            pltpu.VMEM((1, C), F32),
            pltpu.VMEM((9 * C, 3 * C), BF16),
            pltpu.VMEM((9 * C, 3 * C), BF16),
            pltpu.VMEM(((T + 2) * (H + 4) + 8, PITCH, C), F32),
            pltpu.VMEM((T * (H + 2) + 1, PITCH, C), F32),
            pltpu.VMEM((T + 2, H + 4, W, 3 * C), BF16),
            pltpu.VMEM((T + 2, 4 * SIDE, 9 * C), BF16),
            pltpu.VMEM((T, H + 2, W, 3 * C), BF16),
            pltpu.VMEM((T, 4 * H, 9 * C), BF16),
            pltpu.VMEM((T, (H + 2) * W + 4 * SIDE, C), F32),
            pltpu.VMEM((T, H * W + 4 * H, C), F32),
            pltpu.VMEM((2, H, W, C), BF16),
            pltpu.VMEM((2, 4 * H, C), BF16),
            pltpu.VMEM((2, (H - 4) * (W - 4), C), BF16),
            pltpu.VMEM((2, 4 * W + 4 * H, C), BF16),
            pltpu.VMEM((2, (H - 4) * (W - 4), C), BF16),
            pltpu.VMEM((2, 4 * W + 4 * H, C), BF16),
            pltpu.VMEM((4, 16, C), F32),
            pltpu.VMEM((2, (H - 4) * (W - 4), C), F32),
        ]
        + [pltpu.VMEM(shape, BF16) for shape in rims * 2 + [(2, 2, 2, W, C), (6, 4 * H, C)]]
        + [
            pltpu.SemaphoreType.DMA((T + 8,)),
            pltpu.SemaphoreType.DMA((6,)),
            pltpu.SemaphoreType.DMA((6,)),
            pltpu.SemaphoreType.DMA((2, len(DIRS))),
            pltpu.SemaphoreType.DMA((2, len(DIRS))),
            pltpu.SemaphoreType.REGULAR((len(DIRS),)),
        ],
        compiler_params=pltpu.CompilerParams(collective_id=0, has_side_effects=True, vmem_limit_bytes=60 * 2**20),
    )(
        frames,
        gain_first.reshape(1, C),
        weight_first.reshape(3, 9 * C, C),
        gain_second.reshape(1, C),
        weight_second.reshape(3, 9 * C, C),
    )


def solution(mesh):
    sizes = dict(mesh.shape)
    return jax.shard_map(
        functools.partial(block, sizes),
        mesh=mesh,
        in_specs=(P("tm", "row", "col", None), P(), P(), P(), P()),
        out_specs=P("tm", "row", "col", None),
        check_vma=False,
    )
```
